128 devices in a mesh: seq: 32 (over z, x, core), head: 4 (over y).
Axes of the slice: x: 4, y: 4, z: 4, core: 2. Of those that a mesh axis runs over, the one named last changes fastest.
Arguments:
- values_in: bfloat16 [16384, 16384], P(('seq', 'head')), may hold values from -6 to 6
- factors_in: bfloat16 [16384, 8, 2, 256], P(('seq', 'head')), may hold values from -6 to 6
- step_raw: bfloat16 [16384, 256], P(('seq', 'head')), may hold values from -16 to 0
- gate_in: bfloat16 [16384, 16384], P(('seq', 'head')), may hold values from -100 to 100
- conv_values: bfloat16 [4, 16384], replicated, may hold values from -3 to 3
- conv_factors: bfloat16 [4, 8, 2, 256], replicated, may hold values from -3 to 3
- decay_log: float32 [256], replicated, may hold values from -0.3 to 0.3
- skip_gain: float32 [256], replicated, may hold values from 0.5 to 1.5
- norm_gain: float32 [16384], replicated, may hold values from 0.5 to 1.5
Outputs:
- mixed_out: bfloat16 [16384, 16384], P(('seq', 'head'))
The draws below stay inside these ranges and needn't reach their ends.
All inputs are finite; a program needn't handle non-finite values.
Results may differ from the reference program's by a relative error of at most 0.0055.
Values may be sent and summed in bfloat16 or wider, within the bound.
A program may use at most 448 MiB of HBM per device.

```python
import math
from functools import partial
import jax
import jax.numpy as jnp
from jax import lax

SCAN_HEADS = 256
HEAD_DIM = 64
STATE = 256
GROUPS = 8
SPAN = 128
CONV = 4
SEQUENCE_LENGTH = 16384
INNER = 16384


def draw_step_raw(key, part):
    key = jax.random.fold_in(key, 11)
    spike_flags = jax.random.randint(jax.random.fold_in(key, 501), (3,), 0, SEQUENCE_LENGTH)
    first, second, third, fourth_quarter = jax.random.split(key, 4)
    fast_share = 0.25
    medium_share = 0.25
    class_pick = jax.random.uniform(first, (SCAN_HEADS,))
    level_pick = jax.random.uniform(second, (SCAN_HEADS,))
    fast_steps = jnp.exp(math.log(0.02) + level_pick * math.log(2.0))
    medium_steps = jnp.exp(math.log(2.0) + level_pick * math.log(32.0)) / SEQUENCE_LENGTH
    chain_steps = jnp.exp(level_pick * math.log(1.6)) / SEQUENCE_LENGTH
    baseline_steps = jnp.where(class_pick < fast_share, fast_steps, jnp.where(class_pick < fast_share + medium_share, medium_steps, chain_steps))
    small_noise = jnp.exp(jax.random.uniform(third, (SEQUENCE_LENGTH, SCAN_HEADS), minval=-0.35, maxval=0.35))
    spike_steps = jax.random.uniform(fourth_quarter, (SEQUENCE_LENGTH, SCAN_HEADS), minval=0.2, maxval=0.35)
    spike_hits = jnp.any(jnp.arange(SEQUENCE_LENGTH)[:, None] == spike_flags[None, :], axis=1)
    combined_steps = jnp.where(spike_hits[:, None], spike_steps, baseline_steps[None, :] * small_noise)
    return jnp.log(jnp.expm1(combined_steps)).astype(jnp.bfloat16)


def draw_gate_in(key, part):
    key = jax.random.fold_in(key, 23)
    first, second, third = jax.random.split(key, 3)
    column_scale = jnp.exp(jax.random.uniform(first, (1, INNER), minval=0.0, maxval=math.log(10.0)))
    row_scale = jnp.exp(jax.random.uniform(second, (SEQUENCE_LENGTH, 1), minval=0.0, maxval=math.log(10.0)))
    base_values = jnp.clip(jax.random.normal(third, (SEQUENCE_LENGTH, INNER)), -3.0, 3.0)
    return (base_values * column_scale * row_scale / 3.0).astype(jnp.bfloat16)


def block_scale(rng, shape, cuts, least, high):
    gain, own = 1.0, jax.random.fold_in(rng, 6)
    for position, blocks in cuts:
        heights = jnp.exp(jax.random.uniform(jax.random.fold_in(own, position), (blocks,), jnp.float32, least / len(cuts), high / len(cuts)))
        gain = gain * jnp.repeat(heights, shape[position] // blocks).reshape([-1 if axis == position else 1 for axis in range(len(shape))])
    return gain


def centred(rng, dims, deviation, reach, cuts=(), kind=jnp.bfloat16):
    array = jax.random.normal(rng, dims, jnp.float32) * deviation
    if len(cuts) > 0:
        array = block_scale(rng, dims, cuts, -0.22, 0.18) * array
    return jnp.clip(array, min=-reach, max=reach).astype(kind)


def setup_inputs(seed: int = 0) -> dict:
    arg_keys = jax.random.split(jax.random.key(seed), 10)
    return {
        "values_in": centred(arg_keys[0], (SEQUENCE_LENGTH, INNER), 1.0, 6.0, ((0, 128),)),
        "factors_in": centred(arg_keys[1], (SEQUENCE_LENGTH, GROUPS, 2, STATE), 1.0, 6.0, ((0, 128),)),
        "step_raw": draw_step_raw(jax.random.fold_in(arg_keys[9], 71), 0),
        "gate_in": draw_gate_in(jax.random.fold_in(arg_keys[9], 71), 0),
        "conv_values": centred(arg_keys[4], (CONV, INNER), CONV ** -0.5, 3.0),
        "conv_factors": centred(arg_keys[5], (CONV, GROUPS, 2, STATE), CONV ** -0.5, 3.0),
        "decay_log": jnp.clip(jax.random.uniform(arg_keys[6], (SCAN_HEADS,), jnp.float32, -0.3, 0.3), -0.3, 0.3),
        "skip_gain": jnp.clip(jax.random.uniform(arg_keys[7], (SCAN_HEADS,), jnp.float32, 0.5, 1.5), 0.5, 1.5),
        "norm_gain": jnp.clip(1.0 + 0.1 * jax.random.normal(arg_keys[8], (INNER,), jnp.float32), 0.5, 1.5),
    }


def rounded(value):
    return lax.optimization_barrier(value.astype(jnp.bfloat16)).astype(jnp.float32)

def convolve(current, before_rows, weight):
    tap_count = weight.shape[0]
    row_count = current.shape[0]
    padded = jnp.concatenate([before_rows, current], axis=0)
    summed = jnp.zeros(current.shape, jnp.float32)
    for offset in range(tap_count):
        summed = summed + padded[offset:offset + row_count].astype(jnp.float32) * weight[offset].astype(jnp.float32)
    return jax.nn.silu(summed).astype(jnp.bfloat16)

def block_output(decay_rate, skip_local, state_in, blocks):
    signal, b_factor, c_factor, step_sizes = blocks
    row_count = signal.shape[0]
    running = jnp.cumsum(-step_sizes * decay_rate, axis=0)
    scores = jnp.einsum('tgn,sgn->gts', c_factor.astype(jnp.float32), b_factor.astype(jnp.float32))
    causal = jnp.arange(row_count)[:, None] >= jnp.arange(row_count)[None, :]
    running_heads = jnp.transpose(running, (1, 2, 0))
    spacing = jnp.where(causal, running_heads[..., :, None] - running_heads[..., None, :], 0.0)
    step_heads = jnp.transpose(step_sizes, (1, 2, 0))
    mixing = rounded(jnp.where(causal, jnp.exp(spacing) * step_heads[..., None, :] * scores[:, None], 0.0))
    within = jnp.einsum('gjts,sgjp->tgjp', mixing, signal.astype(jnp.float32))
    weights_end = jnp.exp(running[-1] - running) * step_sizes
    weighted = rounded(weights_end[..., None] * signal.astype(jnp.float32))
    fresh_state = jnp.einsum('sgjp,sgn->gjpn', weighted, b_factor.astype(jnp.float32))
    from_state = jnp.einsum('tgn,gjpn->tgjp', c_factor.astype(jnp.float32), rounded(state_in))
    result = within + jnp.exp(running)[..., None] * from_state + skip_local[..., None] * signal.astype(jnp.float32)
    new_state = jnp.exp(running[-1])[..., None, None] * state_in + fresh_state
    return (new_state, result.astype(jnp.bfloat16))

def gated_norm(outputs, gate_values, gain_row, norm_parts):
    row_total = outputs.shape[0]
    gated_values = outputs.astype(jnp.float32) * jax.nn.silu(gate_values.astype(jnp.float32))
    grouped = gated_values.reshape(row_total, norm_parts, -1)
    inverse_rms = lax.rsqrt(lax.optimization_barrier(jnp.mean(grouped * grouped, axis=-1, keepdims=True)) + 1e-05)
    return ((grouped * inverse_rms).reshape(row_total, -1) * gain_row).astype(jnp.bfloat16)

def reference(values_in, factors_in, step_raw, gate_in, conv_values, conv_factors, decay_log, skip_gain, norm_gain):
    margin = CONV - 1
    signal_all = convolve(values_in, jnp.zeros((margin, INNER), jnp.bfloat16), conv_values)
    factor_all = convolve(factors_in, jnp.zeros((margin, GROUPS, 2, STATE), jnp.bfloat16), conv_factors)
    per_group = SCAN_HEADS // GROUPS
    blocks = SEQUENCE_LENGTH // SPAN
    step_sizes = jax.nn.softplus(step_raw.astype(jnp.float32)).reshape(blocks, SPAN, GROUPS, per_group)
    signal_blocks = signal_all.reshape(blocks, SPAN, GROUPS, per_group, HEAD_DIM)
    b_factor = factor_all[:, :, 0].reshape(blocks, SPAN, GROUPS, STATE)
    c_factor = factor_all[:, :, 1].reshape(blocks, SPAN, GROUPS, STATE)
    decay_rate = jnp.exp(decay_log).reshape(GROUPS, per_group)
    skip_local = skip_gain.reshape(GROUPS, per_group)
    empty_state = jnp.zeros((GROUPS, per_group, HEAD_DIM, STATE), jnp.float32)
    final_state, outputs = lax.scan(partial(block_output, decay_rate, skip_local), empty_state, (signal_blocks, b_factor, c_factor, step_sizes))
    outputs = outputs.reshape(SEQUENCE_LENGTH, INNER)
    return gated_norm(outputs, gate_in, norm_gain, GROUPS)
```

```python
from functools import partial

import jax
import jax.numpy as jnp
from jax import lax
from jax.experimental import pallas as pl
from jax.experimental.pallas import tpu as pltpu
from jax.sharding import PartitionSpec as P

HEAD_DIM = 64
STATE = 256
GROUPS = 8
SPAN = 128
CONV = 4
CHUNKS = 4
AHEAD = 2
LANES = 256
F32 = jnp.float32
BF16 = jnp.bfloat16
MESH = pl.DeviceIdType.MESH


def silu(value):
    return value * pl.reciprocal(1.0 + jnp.exp(-value))


def silu_wide(value):
    inner = value * pl.reciprocal(1.0 + jnp.exp(jnp.minimum(-value, 87.0)))
    return jnp.where(value < -87.0, 0.0, inner)


def softplus_below_zero(value):
    e = jnp.exp(value)
    z = e / (2.0 + e)
    q = z * z
    series = 1.0 / 15.0
    for odd in (13.0, 11.0, 9.0, 7.0, 5.0, 3.0, 1.0):
        series = series * q + 1.0 / odd
    return 2.0 * z * series


def split_columns(rows):
    heads = rows.shape[0]
    high = rows.astype(BF16).astype(F32)
    middle = (rows - high).astype(BF16).astype(F32)
    low = rows - high - middle
    parts = [high, middle, low]
    if 128 > 3 * heads:
        parts.append(jnp.zeros((128 - 3 * heads, rows.shape[1]), F32))
    return jnp.transpose(jnp.concatenate(parts, axis=0)).astype(BF16)


def convolved(current, before, taps):
    padded = jnp.concatenate([before, current], axis=0)
    total = padded[5 : 5 + SPAN] * taps[0:1]
    for offset in range(1, CONV):
        total = total + padded[5 + offset : 5 + offset + SPAN] * taps[offset : offset + 1]
    return silu(total).astype(BF16)


def body(
    values_hbm, gate_hbm, fac_in, step_in, halo_in, conv_v, conv_f, decay, skip, gain,
    out_hbm,
    vals, gate, halo_rx, halo_v, halo_f,
    sig_send, sig_recv, fac_send, fac_recv, stp_recv,
    step_t, run_t, run_c, w_s, t_s, g_s, b_t, scores, expander,
    state, local_entry, s_send, st_recv, e_send, e_recv, d_recv, d_wide,
    part, weighted, gated, squares, y_recv,
    val_sem, gate_sem, out_sem, halo_sem,
    sig_ss, sig_rs, fac_ss, fac_rs, stp_ss, stp_rs, d_ss, d_rs,
    st_ss, st_rs, e_ss, e_rs, y_ss, y_rs,
    *, heads, supers,
):
    channels = heads * HEAD_DIM
    width = channels // CHUNKS
    chunk_heads = heads // CHUNKS
    slice_rows = STATE // supers
    lanes = min(LANES, width)

    seq, col = lax.axis_index("seq"), lax.axis_index("head")
    core = lax.rem(seq, 2)
    mine = seq // 2
    me = core * 4 + col
    place = mine * GROUPS + me

    def owner(k):
        return (mine * 2 + k // 4, lax.rem(k, 4))

    def column(j):
        return (j * 2 + core, col)

    def anywhere(index):
        k = lax.rem(index, GROUPS)
        return ((index // GROUPS) * 2 + k // 4, lax.rem(k, 4))

    def other(j):
        return lax.rem(me + j, GROUPS)

    def other_super(j):
        return lax.rem(mine + j, supers)

    total_places = supers * GROUPS
    after = anywhere(lax.rem(place + 1, total_places))
    before = anywhere(lax.rem(place + total_places - 1, total_places))

    def val_copy(g):
        columns = pl.ds(pl.multiple_of(g * channels, channels), channels)
        return pltpu.make_async_copy(values_hbm.at[:, columns], vals.at[:, columns], val_sem.at[g])

    gate_copy = pltpu.make_async_copy(gate_hbm, gate, gate_sem)

    @pl.loop(0, GROUPS)
    def _(j):
        val_copy(other(j + 1)).start()

    gate_copy.start()

    def remote(src, dst, ss, rs, device):
        return pltpu.make_async_remote_copy(
            src_ref=src, dst_ref=dst, send_sem=ss, recv_sem=rs, device_id=device, device_id_type=MESH
        )

    halo_copy = remote(halo_in, halo_rx, halo_sem.at[0], halo_sem.at[1], after)

    def sig_out(g, c):
        return remote(sig_send.at[g, c], sig_recv.at[me, c], sig_ss.at[g, c], sig_rs.at[me, c], owner(g))

    def sig_in(k, c):
        return remote(sig_send.at[k, c], sig_recv.at[k, c], sig_ss.at[k, c], sig_rs.at[k, c], owner(k))

    def fac_out(g):
        return remote(fac_send.at[g], fac_recv.at[me], fac_ss.at[g], fac_rs.at[me], owner(g))

    def fac_arrive(k):
        return remote(fac_send.at[k], fac_recv.at[k], fac_ss.at[k], fac_rs.at[k], owner(k))

    def stp_out(g):
        return remote(step_in.at[g], stp_recv.at[me], stp_ss.at[g], stp_rs.at[me], owner(g))

    def stp_arrive(k):
        return remote(step_in.at[k], stp_recv.at[k], stp_ss.at[k], stp_rs.at[k], owner(k))

    def d_out(j):
        return remote(
            g_s.at[GROUPS - 1, pl.ds(SPAN - 16, 16)], d_recv.at[mine], d_ss.at[j], d_rs.at[mine], column(j)
        )

    def d_arrive(j):
        return remote(
            g_s.at[GROUPS - 1, pl.ds(SPAN - 16, 16)], d_recv.at[j], d_ss.at[j], d_rs.at[j], column(j)
        )

    def part_of(j):
        return pl.ds(pl.multiple_of(j * slice_rows, slice_rows), slice_rows)

    def st_out(j, c):
        return remote(
            s_send.at[c, part_of(j)], st_recv.at[c, mine], st_ss.at[c, j], st_rs.at[c, mine], column(j)
        )

    def st_arrive(j, c):
        return remote(s_send.at[c, part_of(j)], st_recv.at[c, j], st_ss.at[c, j], st_rs.at[c, j], column(j))

    def e_out(j, c):
        return remote(
            e_send.at[c, j], e_recv.at[c, part_of(mine)], e_ss.at[c, j], e_rs.at[c, mine], column(j)
        )

    def e_arrive(j, c):
        return remote(e_send.at[c, j], e_recv.at[c, part_of(j)], e_ss.at[c, j], e_rs.at[c, j], column(j))

    def y_out(k, c):
        return remote(sig_send.at[k, c], y_recv.at[me, c], y_ss.at[k, c], y_rs.at[me, c], owner(k))

    def y_arrive(k, c):
        return remote(sig_send.at[k, c], y_recv.at[k, c], y_ss.at[k, c], y_rs.at[k, c], owner(k))

    barrier = pltpu.get_barrier_semaphore()

    @pl.loop(1, GROUPS)
    def _(j):
        pl.semaphore_signal(barrier, inc=1, device_id=owner(other(j)), device_id_type=MESH)

    @pl.loop(1, supers)
    def _(j):
        pl.semaphore_signal(barrier, inc=1, device_id=column(other_super(j)), device_id_type=MESH)

    pl.semaphore_signal(barrier, inc=1, device_id=after, device_id_type=MESH)
    pl.semaphore_signal(barrier, inc=1, device_id=before, device_id_type=MESH)
    pl.semaphore_wait(barrier, GROUPS - 1 + supers - 1 + 2)

    halo_copy.start()

    @pl.loop(1, GROUPS)
    def _(j):
        stp_out(other(j)).start()

    stp_recv[me] = step_in[me]

    slot = lax.broadcasted_iota(jnp.int32, (128, channels), 0)
    channel = lax.broadcasted_iota(jnp.int32, (128, channels), 1)
    hit = jnp.zeros((128, channels), F32)
    for piece in range(3):
        hit = jnp.where(slot == channel // HEAD_DIM + piece * heads, 1.0, hit)
    expander[...] = hit.astype(BF16)

    def expand(columns, c, lb):
        return jnp.dot(
            columns, expander[:, c * width + lb : c * width + lb + lanes], preferred_element_type=F32
        )

    halo_copy.wait_recv()
    arrived = jnp.where(place > 0, halo_rx[...].astype(F32), 0.0)
    quarter = GROUPS * channels // 4
    quarter_f = GROUPS * 2 * STATE // 4
    for row in range(1, CONV):
        for q in range(4):
            line = arrived[row * 4 + q : row * 4 + q + 1]
            halo_v[4 + row : 5 + row, q * quarter : (q + 1) * quarter] = line[:, :quarter]
            halo_f[4 + row : 5 + row, q * quarter_f : (q + 1) * quarter_f] = line[:, quarter:]

    def factors_of(g, target):
        for lb in range(0, 2 * STATE, LANES):
            here = pl.ds(pl.multiple_of(g * (2 * STATE) + lb, LANES), LANES)
            target[:, lb : lb + LANES] = convolved(
                fac_in[g, :, lb : lb + LANES].astype(F32), halo_f[:, here], conv_f[:, here]
            )

    @pl.loop(1, GROUPS)
    def _(j):
        g = other(j)
        factors_of(g, fac_send.at[g])
        fac_out(g).start()

    factors_of(me, fac_recv.at[me])

    def signal_of(g, c, target):
        @pl.loop(0, width // lanes)
        def _(i):
            lb = pl.multiple_of(i * lanes, lanes)
            here = pl.ds(pl.multiple_of(g * channels + c * width + lb, lanes), lanes)
            target[:, pl.ds(lb, lanes)] = convolved(
                vals[:, here].astype(F32), halo_v[:, here], conv_v[:, here]
            )

    def signals(c, send):
        @pl.loop(1, GROUPS)
        def _(j):
            g = other(j)
            if c == 0:
                val_copy(g).wait()
            signal_of(g, c, sig_send.at[g, c])
            if send:
                sig_out(g, c).start()

        if c == 0:
            val_copy(me).wait()
        signal_of(me, c, sig_recv.at[me, c])

    for c in range(AHEAD):
        signals(c, True)

    @pl.loop(1, GROUPS)
    def _(j):
        stp_arrive(other(j)).wait_recv()

    steps = softplus_below_zero(stp_recv[...].astype(F32))
    step_t[...] = steps
    falls = (steps * jnp.exp(decay[me])[None]).reshape(GROUPS * heads, SPAN)
    upto = (
        lax.broadcasted_iota(jnp.int32, (SPAN, SPAN), 0)
        <= lax.broadcasted_iota(jnp.int32, (SPAN, SPAN), 1)
    ).astype(F32)
    run_t[...] = -jnp.dot(
        falls, upto, preferred_element_type=F32, precision=lax.Precision.HIGHEST
    ).reshape(GROUPS, heads, SPAN)

    def columns_of(k, prior):
        running = run_t[k]
        ending = running[:, SPAN - 1 : SPAN]
        w_s[k] = split_columns(jnp.exp(ending - running) * step_t[k])
        t_s[k] = split_columns(jnp.exp(running))
        g_s[k] = split_columns(jnp.exp(running + prior))
        run_c[k] = jnp.transpose(
            jnp.concatenate([running, jnp.zeros((128 - heads, SPAN), F32)], axis=0)
        )
        return prior + ending

    lax.fori_loop(0, GROUPS, columns_of, jnp.zeros((heads, 1), F32))

    @pl.loop(1, supers)
    def _(j):
        d_out(other_super(j)).start()

    d_recv[mine] = g_s[GROUPS - 1, SPAN - 16 : SPAN, :]

    @pl.loop(1, GROUPS)
    def _(j):
        fac_arrive(other(j)).wait_recv()

    causal = lax.broadcasted_iota(jnp.int32, (SPAN, SPAN), 0) >= lax.broadcasted_iota(
        jnp.int32, (SPAN, SPAN), 1
    )

    @pl.loop(0, GROUPS)
    def _(k):
        b_rows = fac_recv[k, :, 0:STATE]
        turned = jnp.transpose(b_rows.astype(F32)).astype(BF16)
        b_t[k] = turned
        scores[k] = jnp.where(
            causal, jnp.dot(fac_recv[k, :, STATE:], turned, preferred_element_type=F32), 0.0
        )

    for c in range(AHEAD, CHUNKS):
        signals(c, False)

    def wait_chunk(c):
        @pl.loop(1, GROUPS)
        def _(j):
            sig_out(other(j), c).wait_send()
            if c + AHEAD < CHUNKS:
                sig_out(other(j), c + AHEAD).start()

        @pl.loop(1, GROUPS)
        def _(j):
            sig_in(other(j), c).wait_recv()

    def accumulate(c):
        state[...] = jnp.zeros_like(state)

        @pl.loop(0, GROUPS)
        def _(k):
            for lb in range(0, width, lanes):
                here = slice(lb, lb + lanes)
                weight = expand(w_s[k], c, lb)
                weighted[:, here] = (weight * sig_recv[k, c, :, here].astype(F32)).astype(BF16)
                ending = expand(t_s[k, SPAN - 16 : SPAN, :], c, lb)[15:16]
                held = state[:, here]
                local_entry[k, :, here] = held.astype(BF16)
                state[:, here] = held * ending + jnp.dot(
                    b_t[k], weighted[:, here], preferred_element_type=F32
                )

        s_send[c] = state[...].astype(BF16)

        @pl.loop(1, supers)
        def _(j):
            st_out(other_super(j), c).start()

        st_recv[c, mine] = s_send[c, part_of(mine), :]

    def inside(c):
        low_half = lax.broadcasted_iota(jnp.int32, (SPAN, 128), 1) < HEAD_DIM

        @pl.loop(0, GROUPS)
        def _(k):
            for pair in range(chunk_heads // 2):
                here = slice(pair * 128, pair * 128 + 128)
                there = slice(c * width + pair * 128, c * width + pair * 128 + 128)
                mixes = []
                for h in (c * chunk_heads + 2 * pair, c * chunk_heads + 2 * pair + 1):
                    gap = run_c[k, :, h : h + 1] - run_t[k, h : h + 1, :]
                    mixes.append(
                        (jnp.exp(jnp.minimum(gap, 0.0)) * step_t[k, h : h + 1, :] * scores[k]).astype(BF16)
                    )
                signal = sig_recv[k, c, :, here].astype(F32)
                both = jnp.concatenate(
                    [
                        jnp.where(low_half, signal, 0.0).astype(BF16),
                        jnp.where(low_half, 0.0, signal).astype(BF16),
                    ],
                    axis=0,
                )
                part[k, :, there] = (
                    jnp.dot(jnp.concatenate(mixes, axis=1), both, preferred_element_type=F32)
                    + skip[me, :, there] * signal
                )
            for lb in range(0, width, lanes):
                there = slice(c * width + lb, c * width + lb + lanes)
                held = jnp.dot(
                    fac_recv[k, :, STATE:], local_entry[k, :, lb : lb + lanes], preferred_element_type=F32
                )
                part[k, :, there] = part[k, :, there] + expand(t_s[k], c, lb) * held

    def exchange(c):
        if c == 0:

            @pl.loop(1, supers)
            def _(j):
                d_arrive(other_super(j)).wait_recv()

            for j in range(supers):
                d_wide[j : j + 1, :] = jnp.dot(
                    d_recv[j], expander[...], preferred_element_type=F32
                )[15:16]

        @pl.loop(1, supers)
        def _(j):
            st_arrive(other_super(j), c).wait_recv()

        entry = jnp.zeros((slice_rows, width), F32)
        for j in range(supers):
            e_send[c, j] = entry.astype(BF16)
            if j + 1 < supers:
                entry = entry * d_wide[j : j + 1, c * width : (c + 1) * width] + st_recv[c, j].astype(F32)

        @pl.loop(1, supers)
        def _(j):
            e_out(other_super(j), c).start()

        e_recv[c, part_of(mine), :] = e_send[c, mine]

    def results(c):
        @pl.loop(1, supers)
        def _(j):
            e_arrive(other_super(j), c).wait_recv()

        def result_of(k, target):
            for lb in range(0, width, lanes):
                there = slice(c * width + lb, c * width + lb + lanes)
                held = jnp.dot(
                    fac_recv[k, :, STATE:], e_recv[c, :, lb : lb + lanes], preferred_element_type=F32
                )
                target[:, lb : lb + lanes] = (
                    part[k, :, there] + expand(g_s[k], c, lb) * held
                ).astype(BF16)

        @pl.loop(1, GROUPS)
        def _(j):
            k = other(j)
            result_of(k, sig_send.at[k, c])
            y_out(k, c).start()

        result_of(me, y_recv.at[me, c])

    def out_copy(k):
        columns = pl.ds(pl.multiple_of(k * channels, channels), channels)
        return pltpu.make_async_copy(vals.at[:, columns], out_hbm.at[:, columns], out_sem.at[k])

    def finish(c):
        if c == 0:
            gate_copy.wait()

        @pl.loop(0, GROUPS)
        def _(j):
            k = other(j)

            @pl.when(j > 0)
            def _():
                y_arrive(k, c).wait_recv()

            total = jnp.zeros((SPAN, 128), F32)
            if c > 0:
                total = squares[k]
            for lb in range(0, width, lanes):
                here = pl.ds(pl.multiple_of(k * channels + c * width + lb, lanes), lanes)
                value = y_recv[k, c, :, lb : lb + lanes].astype(F32) * silu_wide(
                    gate[:, here].astype(F32)
                )
                gated[k, :, c * width + lb : c * width + lb + lanes] = value
                square = value * value
                for start in range(0, lanes, 128):
                    total = total + square[:, start : start + 128]
            if c + 1 < CHUNKS:
                squares[k] = total
            else:
                mean = jnp.sum(total, axis=1, keepdims=True) * (1.0 / channels)
                inverse = lax.rsqrt(mean + 1e-05)
                for lb in range(0, channels, LANES):
                    here = pl.ds(pl.multiple_of(k * channels + lb, LANES), LANES)
                    vals[:, here] = (
                        gated[k, :, lb : lb + LANES] * inverse * gain[k, :, lb : lb + LANES]
                    ).astype(BF16)
                out_copy(k).start()

    wait_chunk(0)
    accumulate(0)
    inside(0)
    exchange(0)
    for c in range(1, CHUNKS):
        wait_chunk(c)
        accumulate(c)
        results(c - 1)
        inside(c)
        exchange(c)
        if c >= 2:
            finish(c - 2)
    if CHUNKS >= 2:
        finish(CHUNKS - 2)
    results(CHUNKS - 1)
    finish(CHUNKS - 1)

    halo_copy.wait_send()

    @pl.loop(1, GROUPS)
    def _(j):
        g = other(j)
        stp_out(g).wait_send()
        fac_out(g).wait_send()
        for c in range(CHUNKS):
            y_out(g, c).wait_send()

    @pl.loop(1, supers)
    def _(j):
        peer = other_super(j)
        d_out(peer).wait_send()
        for c in range(CHUNKS):
            st_out(peer, c).wait_send()
            e_out(peer, c).wait_send()

    @pl.loop(0, GROUPS)
    def _(j):
        out_copy(other(j)).wait()


def local(
    values_in, factors_in, step_raw, gate_in, conv_values, conv_factors, decay_log, skip_gain, norm_gain
):
    rows, inner = values_in.shape
    heads = step_raw.shape[1] // GROUPS
    channels = heads * HEAD_DIM
    width = channels // CHUNKS
    supers = lax.axis_size("seq") // 2
    slice_rows = STATE // supers
    wide = GROUPS * 2 * STATE

    fac = jnp.transpose(factors_in.reshape(rows, GROUPS, 2 * STATE), (1, 0, 2))
    step_in = jnp.transpose(step_raw).reshape(GROUPS, heads, rows)
    halo = jnp.concatenate(
        [
            values_in[rows - 4 :].reshape(16, inner // 4),
            factors_in[rows - 4 :].reshape(16, wide // 4),
        ],
        axis=1,
    )
    conv_v = conv_values.astype(F32)
    conv_f = conv_factors.reshape(CONV, wide).astype(F32)
    decay = jnp.broadcast_to(decay_log.reshape(GROUPS, heads, 1), (GROUPS, heads, SPAN))
    skip = jnp.repeat(skip_gain, HEAD_DIM).reshape(GROUPS, 1, channels)
    gain = norm_gain.reshape(GROUPS, 1, channels)

    vmem = pl.BlockSpec(memory_space=pltpu.VMEM)
    hbm = pl.BlockSpec(memory_space=pl.ANY)
    dma = pltpu.SemaphoreType.DMA
    scratch = [
        pltpu.VMEM((SPAN, inner), BF16),
        pltpu.VMEM((SPAN, inner), BF16),
        pltpu.VMEM(halo.shape, BF16),
        pltpu.VMEM((8, inner), F32),
        pltpu.VMEM((8, wide), F32),
        pltpu.VMEM((GROUPS, CHUNKS, SPAN, width), BF16),
        pltpu.VMEM((GROUPS, CHUNKS, SPAN, width), BF16),
        pltpu.VMEM((GROUPS, SPAN, 2 * STATE), BF16),
        pltpu.VMEM((GROUPS, SPAN, 2 * STATE), BF16),
        pltpu.VMEM((GROUPS, heads, SPAN), BF16),
        pltpu.VMEM((GROUPS, heads, SPAN), F32),
        pltpu.VMEM((GROUPS, heads, SPAN), F32),
        pltpu.VMEM((GROUPS, SPAN, 128), F32),
        pltpu.VMEM((GROUPS, SPAN, 128), BF16),
        pltpu.VMEM((GROUPS, SPAN, 128), BF16),
        pltpu.VMEM((GROUPS, SPAN, 128), BF16),
        pltpu.VMEM((GROUPS, STATE, SPAN), BF16),
        pltpu.VMEM((GROUPS, SPAN, SPAN), F32),
        pltpu.VMEM((128, channels), BF16),
        pltpu.VMEM((STATE, width), F32),
        pltpu.VMEM((GROUPS, STATE, width), BF16),
        pltpu.VMEM((CHUNKS, STATE, width), BF16),
        pltpu.VMEM((CHUNKS, supers, slice_rows, width), BF16),
        pltpu.VMEM((CHUNKS, supers, slice_rows, width), BF16),
        pltpu.VMEM((CHUNKS, STATE, width), BF16),
        pltpu.VMEM((supers, 16, 128), BF16),
        pltpu.VMEM((max(supers, 8), channels), F32),
        pltpu.VMEM((GROUPS, SPAN, channels), F32),
        pltpu.VMEM((SPAN, width), BF16),
        pltpu.VMEM((GROUPS, SPAN, channels), F32),
        pltpu.VMEM((GROUPS, SPAN, 128), F32),
        pltpu.VMEM((GROUPS, CHUNKS, SPAN, width), BF16),
        dma((GROUPS,)), dma, dma((GROUPS,)), dma((2,)),
        dma((GROUPS, CHUNKS)), dma((GROUPS, CHUNKS)),
        dma((GROUPS,)), dma((GROUPS,)),
        dma((GROUPS,)), dma((GROUPS,)),
        dma((supers,)), dma((supers,)),
        dma((CHUNKS, supers)), dma((CHUNKS, supers)),
        dma((CHUNKS, supers)), dma((CHUNKS, supers)),
        dma((GROUPS, CHUNKS)), dma((GROUPS, CHUNKS)),
    ]
    return pl.pallas_call(
        partial(body, heads=heads, supers=supers),
        out_shape=jax.ShapeDtypeStruct((rows, inner), BF16),
        in_specs=[hbm, hbm] + [vmem] * 8,
        out_specs=hbm,
        scratch_shapes=scratch,
        compiler_params=pltpu.CompilerParams(
            collective_id=0, has_side_effects=True, vmem_limit_bytes=61 * 2**20
        ),
        name="layer",
    )(values_in, gate_in, fac, step_in, halo, conv_v, conv_f, decay, skip, gain)


def solution(mesh):
    rows = P(("seq", "head"), None)
    placed = (rows, P(("seq", "head"), None, None, None), rows, rows, P(), P(), P(), P(), P())
    return jax.shard_map(local, mesh=mesh, in_specs=placed, out_specs=rows, check_vma=False)
```

```python
from functools import partial

import jax
import jax.numpy as jnp
from jax import lax
from jax.experimental import pallas as pl
from jax.experimental.pallas import tpu as pltpu
from jax.sharding import PartitionSpec as P

HEAD_DIM = 64
STATE = 256
GROUPS = 8
SPAN = 128
CONV = 4
CHUNKS = 4
AHEAD = 4
LANES = 256
F32 = jnp.float32
BF16 = jnp.bfloat16
MESH = pl.DeviceIdType.MESH


def silu(value):
    return value * pl.reciprocal(1.0 + jnp.exp(-value))


def silu_wide(value):
    inner = value * pl.reciprocal(1.0 + jnp.exp(jnp.minimum(-value, 87.0)))
    return jnp.where(value < -87.0, 0.0, inner)


def softplus_below_zero(value):
    e = jnp.exp(value)
    z = e / (2.0 + e)
    q = z * z
    series = 1.0 / 15.0
    for odd in (13.0, 11.0, 9.0, 7.0, 5.0, 3.0, 1.0):
        series = series * q + 1.0 / odd
    return 2.0 * z * series


def split_columns(rows):
    heads = rows.shape[0]
    high = rows.astype(BF16).astype(F32)
    middle = (rows - high).astype(BF16).astype(F32)
    low = rows - high - middle
    parts = [high, middle, low]
    if 128 > 3 * heads:
        parts.append(jnp.zeros((128 - 3 * heads, rows.shape[1]), F32))
    return jnp.transpose(jnp.concatenate(parts, axis=0)).astype(BF16)


def convolved(current, before, taps):
    padded = jnp.concatenate([before, current], axis=0)
    total = padded[5 : 5 + SPAN] * taps[0:1]
    for offset in range(1, CONV):
        total = total + padded[5 + offset : 5 + offset + SPAN] * taps[offset : offset + 1]
    return silu(total).astype(BF16)


def body(
    values_hbm, gate_hbm, fac_hbm, step_in, conv_v, conv_f, decay, skip, gain,
    out_hbm,
    out, gate, tail_v, tail_f, raw_v, raw_f, signal, b_rows, c_rows, stp_send, stp_recv,
    head_col, skip_row, step_t, run_t, run_c, w_s, t_s, g_s, b_t, scores, expander,
    state, local_entry, s_send, st_recv, e_send, e_recv, d_recv, d_wide,
    part, weighted, gated, squares, y_send, y_recv,
    own_sem, gate_sem, out_sem, tail_ss, tail_rs,
    sig_ss, sig_rs, fac_ss, fac_rs, stp_ss, stp_rs, d_ss, d_rs,
    st_ss, st_rs, e_ss, e_rs, y_ss, y_rs,
    *, heads, supers,
):
    channels = heads * HEAD_DIM
    width = channels // CHUNKS
    chunk_heads = heads // CHUNKS
    slice_rows = STATE // supers
    lanes = min(LANES, width)

    seq, col = lax.axis_index("seq"), lax.axis_index("head")
    core = lax.rem(seq, 2)
    mine = seq // 2
    me = core * 4 + col
    place = mine * GROUPS + me

    def owner(k):
        return (mine * 2 + k // 4, lax.rem(k, 4))

    def column(j):
        return (j * 2 + core, col)

    def anywhere(index):
        k = lax.rem(index, GROUPS)
        return ((index // GROUPS) * 2 + k // 4, lax.rem(k, 4))

    def other(j):
        return lax.rem(me + j, GROUPS)

    def other_super(j):
        return lax.rem(mine + j, supers)

    following = column(other_super(1))
    previous = column(other_super(supers - 1))

    def columns_of_chunk(g, c):
        return pl.ds(pl.multiple_of(g * channels + c * width, width), width)

    def own_copy(c):
        return pltpu.make_async_copy(
            values_hbm.at[:, columns_of_chunk(me, c)], raw_v.at[me, c], own_sem.at[c]
        )

    own_factors = pltpu.make_async_copy(fac_hbm.at[me], raw_f.at[me], own_sem.at[CHUNKS])
    gate_copy = pltpu.make_async_copy(gate_hbm, gate, gate_sem)

    def remote(src, dst, ss, rs, device):
        return pltpu.make_async_remote_copy(
            src_ref=src, dst_ref=dst, send_sem=ss, recv_sem=rs, device_id=device, device_id_type=MESH
        )

    def sig_out(g, c):
        return remote(
            values_hbm.at[:, columns_of_chunk(g, c)], raw_v.at[me, c], sig_ss.at[g, c], sig_rs.at[me, c], owner(g)
        )

    def sig_in(k, c):
        return remote(
            values_hbm.at[:, columns_of_chunk(k, c)], raw_v.at[k, c], sig_ss.at[k, c], sig_rs.at[k, c], owner(k)
        )

    def fac_out(g):
        return remote(fac_hbm.at[g], raw_f.at[me], fac_ss.at[g], fac_rs.at[me], owner(g))

    def fac_arrive(k):
        return remote(fac_hbm.at[k], raw_f.at[k], fac_ss.at[k], fac_rs.at[k], owner(k))

    last_rows = pl.ds(SPAN - 16, 16)

    def tail_v_copy(c):
        return remote(
            raw_v.at[GROUPS - 1, c, last_rows], tail_v.at[c], tail_ss.at[c], tail_rs.at[c], following
        )

    tail_f_copy = remote(
        raw_f.at[GROUPS - 1, :, last_rows], tail_f, tail_ss.at[CHUNKS], tail_rs.at[CHUNKS], following
    )

    def stp_out(g):
        return remote(stp_send.at[g], stp_recv.at[me], stp_ss.at[g], stp_rs.at[me], owner(g))

    def stp_arrive(k):
        return remote(stp_send.at[k], stp_recv.at[k], stp_ss.at[k], stp_rs.at[k], owner(k))

    def d_out(j):
        return remote(
            g_s.at[GROUPS - 1, pl.ds(SPAN - 16, 16)], d_recv.at[mine], d_ss.at[j], d_rs.at[mine], column(j)
        )

    def d_arrive(j):
        return remote(
            g_s.at[GROUPS - 1, pl.ds(SPAN - 16, 16)], d_recv.at[j], d_ss.at[j], d_rs.at[j], column(j)
        )

    def part_of(j):
        return pl.ds(pl.multiple_of(j * slice_rows, slice_rows), slice_rows)

    def st_out(j, c):
        return remote(
            s_send.at[c, part_of(j)], st_recv.at[c, mine], st_ss.at[c, j], st_rs.at[c, mine], column(j)
        )

    def st_arrive(j, c):
        return remote(s_send.at[c, part_of(j)], st_recv.at[c, j], st_ss.at[c, j], st_rs.at[c, j], column(j))

    def e_out(j, c):
        return remote(
            e_send.at[c, j], e_recv.at[c, part_of(mine)], e_ss.at[c, j], e_rs.at[c, mine], column(j)
        )

    def e_arrive(j, c):
        return remote(e_send.at[c, j], e_recv.at[c, part_of(j)], e_ss.at[c, j], e_rs.at[c, j], column(j))

    def y_out(k, c):
        return remote(y_send.at[k, c], y_recv.at[me, c], y_ss.at[k, c], y_rs.at[me, c], owner(k))

    def y_arrive(k, c):
        return remote(y_send.at[k, c], y_recv.at[k, c], y_ss.at[k, c], y_rs.at[k, c], owner(k))

    barrier = pltpu.get_barrier_semaphore()

    @pl.loop(1, GROUPS)
    def _(j):
        pl.semaphore_signal(barrier, inc=1, device_id=owner(other(j)), device_id_type=MESH)

    @pl.loop(1, supers)
    def _(j):
        pl.semaphore_signal(barrier, inc=1, device_id=column(other_super(j)), device_id_type=MESH)

    for start in range(0, GROUPS * heads, 128):
        count = min(128, GROUPS * heads - start)
        turned = jnp.transpose(step_in[:, start : start + count].astype(F32)).astype(BF16)
        stp_send[start // heads : (start + count) // heads] = turned.reshape(count // heads, heads, SPAN)

    pl.semaphore_wait(barrier, GROUPS - 1 + supers - 1)

    @pl.loop(1, GROUPS)
    def _(j):
        stp_out(other(j)).start()

    @pl.loop(1, GROUPS)
    def _(j):
        fac_out(other(j)).start()

    for c in range(AHEAD):

        @pl.loop(1, GROUPS)
        def _(j):
            sig_out(other(j), c).start()

    own_factors.start()
    for c in range(CHUNKS):
        own_copy(c).start()
    gate_copy.start()

    stp_recv[me] = stp_send[me]

    def turn_row(row):
        for start in range(0, GROUPS * heads, 128):
            count = min(128, GROUPS * heads - start)
            head_col[start : start + count, :] = jnp.transpose(
                jnp.broadcast_to(row[:, start : start + count], (128, count))
            )
        return head_col[pl.ds(pl.multiple_of(me * heads, heads), heads), :]

    slot = lax.broadcasted_iota(jnp.int32, (128, channels), 0)
    channel = lax.broadcasted_iota(jnp.int32, (128, channels), 1)
    hit = jnp.zeros((128, channels), F32)
    for piece in range(3):
        hit = jnp.where(slot == channel // HEAD_DIM + piece * heads, 1.0, hit)
    expander[...] = hit.astype(BF16)

    def expand(columns, c, lb):
        return jnp.dot(
            columns, expander[:, c * width + lb : c * width + lb + lanes], preferred_element_type=F32
        )

    skip_columns = split_columns(turn_row(skip))
    for lb in range(0, channels, lanes):
        skip_row[:, lb : lb + lanes] = expand(skip_columns[0:16, :], 0, lb)[0:8]
    rate = jnp.exp(turn_row(decay))

    def tail_before(rows):
        return jnp.where(mine > 0, rows.astype(F32), 0.0)

    def signal_of(k, c, before):
        for lb in range(0, width, lanes):
            here = slice(lb, lb + lanes)
            taps = conv_v[:, pl.ds(pl.multiple_of(me * channels + c * width + lb, lanes), lanes)]
            signal[k, c, :, here] = convolved(
                raw_v[k, c, :, here].astype(F32), before(here), taps.astype(F32)
            )

    def factors_of(k, before):
        for part_index, target in ((0, b_rows), (1, c_rows)):
            taps = conv_f[:, me, part_index, :].astype(F32)
            target[k] = convolved(raw_f[k, part_index].astype(F32), before(part_index), taps)

    @pl.loop(1, GROUPS)
    def _(j):
        stp_arrive(other(j)).wait_recv()

    steps = softplus_below_zero(stp_recv[...].astype(F32))
    step_t[...] = steps
    falls = (steps * rate[None]).reshape(GROUPS * heads, SPAN)
    upto = (
        lax.broadcasted_iota(jnp.int32, (SPAN, SPAN), 0)
        <= lax.broadcasted_iota(jnp.int32, (SPAN, SPAN), 1)
    ).astype(F32)
    run_t[...] = -jnp.dot(
        falls, upto, preferred_element_type=F32, precision=lax.Precision.HIGHEST
    ).reshape(GROUPS, heads, SPAN)

    def columns_of(k, prior):
        running = run_t[k]
        ending = running[:, SPAN - 1 : SPAN]
        w_s[k] = split_columns(jnp.exp(ending - running) * step_t[k])
        t_s[k] = split_columns(jnp.exp(running))
        g_s[k] = split_columns(jnp.exp(running + prior))
        run_c[k] = jnp.transpose(
            jnp.concatenate([running, jnp.zeros((128 - heads, SPAN), F32)], axis=0)
        )
        return prior + ending

    lax.fori_loop(0, GROUPS, columns_of, jnp.zeros((heads, 1), F32))

    @pl.loop(1, supers)
    def _(j):
        d_out(other_super(j)).start()

    d_recv[mine] = g_s[GROUPS - 1, SPAN - 16 : SPAN, :]

    @pl.loop(1, GROUPS)
    def _(j):
        fac_arrive(other(j)).wait_recv()

    own_factors.wait()
    tail_f_copy.start()

    causal = lax.broadcasted_iota(jnp.int32, (SPAN, SPAN), 0) >= lax.broadcasted_iota(
        jnp.int32, (SPAN, SPAN), 1
    )

    def scores_of(k):
        turned = jnp.transpose(b_rows[k].astype(F32)).astype(BF16)
        b_t[k] = turned
        scores[k] = jnp.where(causal, jnp.dot(c_rows[k], turned, preferred_element_type=F32), 0.0)

    @pl.loop(1, GROUPS)
    def _(k):
        factors_of(k, lambda i: raw_f[k - 1, i, SPAN - 16 : SPAN, :].astype(F32)[8:16])
        scores_of(k)

    tail_f_copy.wait_recv()
    factors_of(0, lambda i: tail_before(tail_f[i])[8:16])
    scores_of(0)

    def wait_chunk(c):
        @pl.loop(1, GROUPS)
        def _(j):
            sig_out(other(j), c).wait_send()
            if c + AHEAD < CHUNKS:
                sig_out(other(j), c + AHEAD).start()

        @pl.loop(1, GROUPS)
        def _(j):
            sig_in(other(j), c).wait_recv()

        own_copy(c).wait()
        tail_v_copy(c).start()

        @pl.loop(1, GROUPS)
        def _(k):
            signal_of(k, c, lambda here: raw_v[k - 1, c, SPAN - 16 : SPAN, here].astype(F32)[8:16])

        tail_v_copy(c).wait_recv()
        signal_of(0, c, lambda here: tail_before(tail_v[c, :, here])[8:16])

    def accumulate(c):
        state[...] = jnp.zeros_like(state)

        @pl.loop(0, GROUPS)
        def _(k):
            for lb in range(0, width, lanes):
                here = slice(lb, lb + lanes)
                weight = expand(w_s[k], c, lb)
                weighted[:, here] = (weight * signal[k, c, :, here].astype(F32)).astype(BF16)
                ending = expand(t_s[k, SPAN - 16 : SPAN, :], c, lb)[15:16]
                held = state[:, here]
                local_entry[k, :, here] = held.astype(BF16)
                state[:, here] = held * ending + jnp.dot(
                    b_t[k], weighted[:, here], preferred_element_type=F32
                )

        s_send[c] = state[...].astype(BF16)

        @pl.loop(1, supers)
        def _(j):
            st_out(other_super(j), c).start()

        st_recv[c, mine] = s_send[c, part_of(mine), :]

    def inside(c):
        low_half = lax.broadcasted_iota(jnp.int32, (SPAN, 128), 1) < HEAD_DIM

        @pl.loop(0, GROUPS)
        def _(k):
            for pair in range(chunk_heads // 2):
                here = slice(pair * 128, pair * 128 + 128)
                there = slice(c * width + pair * 128, c * width + pair * 128 + 128)
                mixes = []
                for h in (c * chunk_heads + 2 * pair, c * chunk_heads + 2 * pair + 1):
                    gap = run_c[k, :, h : h + 1] - run_t[k, h : h + 1, :]
                    mixes.append(
                        (jnp.exp(jnp.minimum(gap, 0.0)) * step_t[k, h : h + 1, :] * scores[k]).astype(BF16)
                    )
                values = signal[k, c, :, here].astype(F32)
                both = jnp.concatenate(
                    [
                        jnp.where(low_half, values, 0.0).astype(BF16),
                        jnp.where(low_half, 0.0, values).astype(BF16),
                    ],
                    axis=0,
                )
                part[k, :, there] = (
                    jnp.dot(jnp.concatenate(mixes, axis=1), both, preferred_element_type=F32)
                    + skip_row[0:1, there] * values
                )
            for lb in range(0, width, lanes):
                there = slice(c * width + lb, c * width + lb + lanes)
                held = jnp.dot(
                    c_rows[k], local_entry[k, :, lb : lb + lanes], preferred_element_type=F32
                )
                part[k, :, there] = part[k, :, there] + expand(t_s[k], c, lb) * held

    def exchange(c):
        if c == 0:

            @pl.loop(1, supers)
            def _(j):
                d_arrive(other_super(j)).wait_recv()

            for j in range(supers):
                d_wide[j : j + 1, :] = jnp.dot(
                    d_recv[j], expander[...], preferred_element_type=F32
                )[15:16]

        @pl.loop(1, supers)
        def _(j):
            st_arrive(other_super(j), c).wait_recv()

        entry = jnp.zeros((slice_rows, width), F32)
        for j in range(supers):
            e_send[c, j] = entry.astype(BF16)
            if j + 1 < supers:
                entry = entry * d_wide[j : j + 1, c * width : (c + 1) * width] + st_recv[c, j].astype(F32)

        @pl.loop(1, supers)
        def _(j):
            e_out(other_super(j), c).start()

        e_recv[c, part_of(mine), :] = e_send[c, mine]

    def results(c):
        @pl.loop(1, supers)
        def _(j):
            e_arrive(other_super(j), c).wait_recv()

        def result_of(k, target):
            for lb in range(0, width, lanes):
                there = slice(c * width + lb, c * width + lb + lanes)
                held = jnp.dot(
                    c_rows[k], e_recv[c, :, lb : lb + lanes], preferred_element_type=F32
                )
                target[:, lb : lb + lanes] = (
                    part[k, :, there] + expand(g_s[k], c, lb) * held
                ).astype(BF16)

        @pl.loop(1, GROUPS)
        def _(j):
            k = other(j)
            result_of(k, y_send.at[k, c])
            y_out(k, c).start()

        result_of(me, y_recv.at[me, c])

    def out_copy(k):
        columns = pl.ds(pl.multiple_of(k * channels, channels), channels)
        return pltpu.make_async_copy(out.at[:, columns], out_hbm.at[:, columns], out_sem.at[k])

    def finish(c):
        if c == 0:
            gate_copy.wait()

        @pl.loop(0, GROUPS)
        def _(j):
            k = other(j)

            @pl.when(j > 0)
            def _():
                y_arrive(k, c).wait_recv()

            total = jnp.zeros((SPAN, 128), F32)
            if c > 0:
                total = squares[k]
            for lb in range(0, width, lanes):
                here = pl.ds(pl.multiple_of(k * channels + c * width + lb, lanes), lanes)
                value = y_recv[k, c, :, lb : lb + lanes].astype(F32) * silu_wide(
                    gate[:, here].astype(F32)
                )
                gated[k, :, c * width + lb : c * width + lb + lanes] = value
                square = value * value
                for start in range(0, lanes, 128):
                    total = total + square[:, start : start + 128]
            if c + 1 < CHUNKS:
                squares[k] = total
            else:
                mean = jnp.sum(total, axis=1, keepdims=True) * (1.0 / channels)
                inverse = lax.rsqrt(mean + 1e-05)
                for lb in range(0, channels, LANES):
                    here = pl.ds(pl.multiple_of(k * channels + lb, LANES), LANES)
                    out[:, here] = (
                        gated[k, :, lb : lb + LANES] * inverse * gain[k, :, lb : lb + LANES]
                    ).astype(BF16)
                out_copy(k).start()

    wait_chunk(0)
    accumulate(0)
    inside(0)
    exchange(0)
    for c in range(1, CHUNKS):
        wait_chunk(c)
        accumulate(c)
        results(c - 1)
        inside(c)
        exchange(c)
    results(CHUNKS - 1)
    for c in range(CHUNKS):
        finish(c)

    tail_f_copy.wait_send()
    for c in range(CHUNKS):
        tail_v_copy(c).wait_send()

    @pl.loop(1, GROUPS)
    def _(j):
        g = other(j)
        stp_out(g).wait_send()
        fac_out(g).wait_send()
        for c in range(CHUNKS):
            y_out(g, c).wait_send()

    @pl.loop(1, supers)
    def _(j):
        peer = other_super(j)
        d_out(peer).wait_send()
        for c in range(CHUNKS):
            st_out(peer, c).wait_send()
            e_out(peer, c).wait_send()

    @pl.loop(0, GROUPS)
    def _(j):
        out_copy(other(j)).wait()


def local(
    values_in, factors_in, step_raw, gate_in, conv_values, conv_factors, decay_log, skip_gain, norm_gain
):
    rows, inner = values_in.shape
    heads = step_raw.shape[1] // GROUPS
    channels = heads * HEAD_DIM
    width = channels // CHUNKS
    supers = lax.axis_size("seq") // 2
    slice_rows = STATE // supers

    fac = jnp.transpose(factors_in, (1, 2, 0, 3))
    gain = norm_gain.reshape(GROUPS, 1, channels)

    vmem = pl.BlockSpec(memory_space=pltpu.VMEM)
    hbm = pl.BlockSpec(memory_space=pl.ANY)
    dma = pltpu.SemaphoreType.DMA
    scratch = [
        pltpu.VMEM((SPAN, inner), BF16),
        pltpu.VMEM((SPAN, inner), BF16),
        pltpu.VMEM((CHUNKS, 16, width), BF16),
        pltpu.VMEM((2, 16, STATE), BF16),
        pltpu.VMEM((GROUPS, CHUNKS, SPAN, width), BF16),
        pltpu.VMEM((GROUPS, 2, SPAN, STATE), BF16),
        pltpu.VMEM((GROUPS, CHUNKS, SPAN, width), BF16),
        pltpu.VMEM((GROUPS, SPAN, STATE), BF16),
        pltpu.VMEM((GROUPS, SPAN, STATE), BF16),
        pltpu.VMEM((GROUPS, heads, SPAN), BF16),
        pltpu.VMEM((GROUPS, heads, SPAN), BF16),
        pltpu.VMEM((GROUPS * heads, 128), F32),
        pltpu.VMEM((8, channels), F32),
        pltpu.VMEM((GROUPS, heads, SPAN), F32),
        pltpu.VMEM((GROUPS, heads, SPAN), F32),
        pltpu.VMEM((GROUPS, SPAN, 128), F32),
        pltpu.VMEM((GROUPS, SPAN, 128), BF16),
        pltpu.VMEM((GROUPS, SPAN, 128), BF16),
        pltpu.VMEM((GROUPS, SPAN, 128), BF16),
        pltpu.VMEM((GROUPS, STATE, SPAN), BF16),
        pltpu.VMEM((GROUPS, SPAN, SPAN), F32),
        pltpu.VMEM((128, channels), BF16),
        pltpu.VMEM((STATE, width), F32),
        pltpu.VMEM((GROUPS, STATE, width), BF16),
        pltpu.VMEM((CHUNKS, STATE, width), BF16),
        pltpu.VMEM((CHUNKS, supers, slice_rows, width), BF16),
        pltpu.VMEM((CHUNKS, supers, slice_rows, width), BF16),
        pltpu.VMEM((CHUNKS, STATE, width), BF16),
        pltpu.VMEM((supers, 16, 128), BF16),
        pltpu.VMEM((max(supers, 8), channels), F32),
        pltpu.VMEM((GROUPS, SPAN, channels), F32),
        pltpu.VMEM((SPAN, width), BF16),
        pltpu.VMEM((GROUPS, SPAN, channels), F32),
        pltpu.VMEM((GROUPS, SPAN, 128), F32),
        pltpu.VMEM((GROUPS, CHUNKS, SPAN, width), BF16),
        pltpu.VMEM((GROUPS, CHUNKS, SPAN, width), BF16),
        dma((CHUNKS + 1,)), dma, dma((GROUPS,)), dma((CHUNKS + 1,)), dma((CHUNKS + 1,)),
        dma((GROUPS, CHUNKS)), dma((GROUPS, CHUNKS)),
        dma((GROUPS,)), dma((GROUPS,)),
        dma((GROUPS,)), dma((GROUPS,)),
        dma((supers,)), dma((supers,)),
        dma((CHUNKS, supers)), dma((CHUNKS, supers)),
        dma((CHUNKS, supers)), dma((CHUNKS, supers)),
        dma((GROUPS, CHUNKS)), dma((GROUPS, CHUNKS)),
    ]
    return pl.pallas_call(
        partial(body, heads=heads, supers=supers),
        out_shape=jax.ShapeDtypeStruct((rows, inner), BF16),
        in_specs=[hbm, hbm, hbm] + [vmem] * 6,
        out_specs=hbm,
        scratch_shapes=scratch,
        compiler_params=pltpu.CompilerParams(
            collective_id=0, has_side_effects=True, vmem_limit_bytes=61 * 2**20
        ),
        name="layer",
    )(
        values_in, gate_in, fac, step_raw, conv_values, conv_factors,
        decay_log.reshape(1, -1), skip_gain.reshape(1, -1), gain,
    )


def solution(mesh):
    rows = P(("seq", "head"), None)
    placed = (rows, P(("seq", "head"), None, None, None), rows, rows, P(), P(), P(), P(), P())
    return jax.shard_map(local, mesh=mesh, in_specs=placed, out_specs=rows, check_vma=False)
```

```python
from functools import partial

import jax
import jax.numpy as jnp
from jax import lax
from jax.experimental import pallas as pl
from jax.experimental.pallas import tpu as pltpu
from jax.sharding import PartitionSpec as P

HEAD_DIM = 64
STATE = 256
GROUPS = 8
SPAN = 128
CONV = 4
CHUNKS = 4
AHEAD = 4
LANES = 256
F32 = jnp.float32
BF16 = jnp.bfloat16
MESH = pl.DeviceIdType.MESH


def silu(value):
    return value * pl.reciprocal(1.0 + jnp.exp(-value))


def silu_wide(value):
    inner = value * pl.reciprocal(1.0 + jnp.exp(jnp.minimum(-value, 87.0)))
    return jnp.where(value < -87.0, 0.0, inner)


def softplus_below_zero(value):
    e = jnp.exp(value)
    z = e / (2.0 + e)
    q = z * z
    series = 1.0 / 15.0
    for odd in (13.0, 11.0, 9.0, 7.0, 5.0, 3.0, 1.0):
        series = series * q + 1.0 / odd
    return 2.0 * z * series


def split_columns(rows):
    heads = rows.shape[0]
    high = rows.astype(BF16).astype(F32)
    middle = (rows - high).astype(BF16).astype(F32)
    low = rows - high - middle
    parts = [high, middle, low]
    if 128 > 3 * heads:
        parts.append(jnp.zeros((128 - 3 * heads, rows.shape[1]), F32))
    return jnp.transpose(jnp.concatenate(parts, axis=0)).astype(BF16)


def convolved(current, before, taps):
    padded = jnp.concatenate([before, current], axis=0)
    total = padded[5 : 5 + SPAN] * taps[0:1]
    for offset in range(1, CONV):
        total = total + padded[5 + offset : 5 + offset + SPAN] * taps[offset : offset + 1]
    return silu(total).astype(BF16)


def body(
    values_hbm, gate_hbm, fac_hbm, step_hbm, conv_v_hbm, conv_f_hbm, decay_hbm, skip_hbm, gain_hbm,
    out_hbm,
    step_in, conv_v, conv_f, decay, skip, gain, out, gate, tail_v, tail_f, raw_v, raw_f, signal, b_rows, c_rows, stp_send, stp_recv,
    head_col, skip_row, step_t, run_t, run_c, w_s, t_s, g_s, b_t, scores, expander,
    state, local_entry, s_send, st_recv, e_send, e_recv, d_recv, d_wide,
    part, weighted, gated, squares, y_send, y_recv,
    own_sem, gate_sem, out_sem, tail_ss, tail_rs,
    sig_ss, sig_rs, fac_ss, fac_rs, stp_ss, stp_rs, d_ss, d_rs,
    st_ss, st_rs, e_ss, e_rs, y_ss, y_rs, met, small_sem,
    *, heads, supers,
):
    channels = heads * HEAD_DIM
    width = channels // CHUNKS
    chunk_heads = heads // CHUNKS
    slice_rows = STATE // supers
    lanes = min(LANES, width)

    seq, col = lax.axis_index("seq"), lax.axis_index("head")
    core = lax.rem(seq, 2)
    mine = seq // 2
    me = core * 4 + col
    place = mine * GROUPS + me

    def owner(k):
        return (mine * 2 + k // 4, lax.rem(k, 4))

    def column(j):
        return (j * 2 + core, col)

    def anywhere(index):
        k = lax.rem(index, GROUPS)
        return ((index // GROUPS) * 2 + k // 4, lax.rem(k, 4))

    def other(j):
        return lax.rem(me + j, GROUPS)

    def other_super(j):
        return lax.rem(mine + j, supers)

    following = column(other_super(1))
    previous = column(other_super(supers - 1))

    def columns_of_chunk(g, c):
        return pl.ds(pl.multiple_of(g * channels + c * width, width), width)

    def own_copy(c):
        return pltpu.make_async_copy(
            values_hbm.at[:, columns_of_chunk(me, c)], raw_v.at[me, c], own_sem.at[c]
        )

    own_factors = pltpu.make_async_copy(fac_hbm.at[:, me], raw_f.at[me], own_sem.at[CHUNKS])
    gate_copy = pltpu.make_async_copy(gate_hbm, gate, gate_sem)

    def remote(src, dst, ss, rs, device):
        return pltpu.make_async_remote_copy(
            src_ref=src, dst_ref=dst, send_sem=ss, recv_sem=rs, device_id=device, device_id_type=MESH
        )

    def sig_out(g, c):
        return remote(
            values_hbm.at[:, columns_of_chunk(g, c)], raw_v.at[me, c], sig_ss.at[g, c], sig_rs.at[me, c], owner(g)
        )

    def sig_in(k, c):
        return remote(
            values_hbm.at[:, columns_of_chunk(k, c)], raw_v.at[k, c], sig_ss.at[k, c], sig_rs.at[k, c], owner(k)
        )

    def fac_out(g):
        return remote(fac_hbm.at[:, g], raw_f.at[me], fac_ss.at[g], fac_rs.at[me], owner(g))

    def fac_arrive(k):
        return remote(fac_hbm.at[:, k], raw_f.at[k], fac_ss.at[k], fac_rs.at[k], owner(k))

    last_rows = pl.ds(SPAN - 16, 16)

    def tail_v_copy(c):
        return remote(
            raw_v.at[GROUPS - 1, c, last_rows], tail_v.at[c], tail_ss.at[c], tail_rs.at[c], following
        )

    tail_f_copy = remote(
        raw_f.at[GROUPS - 1, last_rows], tail_f, tail_ss.at[CHUNKS], tail_rs.at[CHUNKS], following
    )

    def stp_out(g):
        return remote(stp_send.at[g], stp_recv.at[me], stp_ss.at[g], stp_rs.at[me], owner(g))

    def stp_arrive(k):
        return remote(stp_send.at[k], stp_recv.at[k], stp_ss.at[k], stp_rs.at[k], owner(k))

    def d_out(j):
        return remote(
            g_s.at[GROUPS - 1, pl.ds(SPAN - 16, 16)], d_recv.at[mine], d_ss.at[j], d_rs.at[mine], column(j)
        )

    def d_arrive(j):
        return remote(
            g_s.at[GROUPS - 1, pl.ds(SPAN - 16, 16)], d_recv.at[j], d_ss.at[j], d_rs.at[j], column(j)
        )

    def part_of(j):
        return pl.ds(pl.multiple_of(j * slice_rows, slice_rows), slice_rows)

    def st_out(j, c):
        return remote(
            s_send.at[c, part_of(j)], st_recv.at[c, mine], st_ss.at[c, j], st_rs.at[c, mine], column(j)
        )

    def st_arrive(j, c):
        return remote(s_send.at[c, part_of(j)], st_recv.at[c, j], st_ss.at[c, j], st_rs.at[c, j], column(j))

    def e_out(j, c):
        return remote(
            e_send.at[c, j], e_recv.at[c, part_of(mine)], e_ss.at[c, j], e_rs.at[c, mine], column(j)
        )

    def e_arrive(j, c):
        return remote(e_send.at[c, j], e_recv.at[c, part_of(j)], e_ss.at[c, j], e_rs.at[c, j], column(j))

    def y_out(k, c):
        return remote(y_send.at[k, c], y_recv.at[me, c], y_ss.at[k, c], y_rs.at[me, c], owner(k))

    def y_arrive(k, c):
        return remote(y_send.at[k, c], y_recv.at[k, c], y_ss.at[k, c], y_rs.at[k, c], owner(k))

    small = [
        pltpu.make_async_copy(source, target, small_sem.at[i])
        for i, (source, target) in enumerate(
            [
                (step_hbm, step_in), (conv_v_hbm, conv_v), (conv_f_hbm, conv_f),
                (decay_hbm, decay), (skip_hbm, skip), (gain_hbm, gain),
            ]
        )
    ]
    small[0].start()
    barrier = pltpu.get_barrier_semaphore()

    @pl.loop(1, GROUPS)
    def _(j):
        pl.semaphore_signal(barrier, inc=1, device_id=owner(other(j)), device_id_type=MESH)

    pairs = [1 << d for d in range(supers.bit_length() - 1)]

    def opposite(pair):
        return column(mine + pair - 2 * pair * lax.rem(mine // pair, 2))

    for pair in pairs:
        pl.semaphore_signal(barrier, inc=1, device_id=opposite(pair), device_id_type=MESH)

    small[0].wait()
    for start in range(0, GROUPS * heads, 128):
        count = min(128, GROUPS * heads - start)
        turned = jnp.transpose(step_in[:, start : start + count].astype(F32)).astype(BF16)
        stp_send[start // heads : (start + count) // heads] = turned.reshape(count // heads, heads, SPAN)

    pl.semaphore_wait(barrier, GROUPS - 1 + len(pairs))

    @pl.loop(1, GROUPS)
    def _(j):
        stp_out(other(j)).start()

    @pl.loop(1, GROUPS)
    def _(j):
        fac_out(other(j)).start()

    for c in range(AHEAD):

        @pl.loop(1, GROUPS)
        def _(j):
            sig_out(other(j), c).start()

    own_factors.start()
    for copy in small[1:]:
        copy.start()
    for c in range(CHUNKS):
        own_copy(c).start()
    gate_copy.start()

    stp_recv[me] = stp_send[me]

    def turn_row(row):
        for start in range(0, GROUPS * heads, 128):
            count = min(128, GROUPS * heads - start)
            head_col[start : start + count, :] = jnp.transpose(
                jnp.broadcast_to(row[:, start : start + count], (128, count))
            )
        return head_col[pl.ds(pl.multiple_of(me * heads, heads), heads), :]

    for d, pair in enumerate(pairs):
        pl.semaphore_signal(met.at[d], inc=1, device_id=opposite(pair), device_id_type=MESH)
        pl.semaphore_wait(met.at[d], 1)

    slot = lax.broadcasted_iota(jnp.int32, (128, channels), 0)
    channel = lax.broadcasted_iota(jnp.int32, (128, channels), 1)
    hit = jnp.zeros((128, channels), F32)
    for piece in range(3):
        hit = jnp.where(slot == channel // HEAD_DIM + piece * heads, 1.0, hit)
    expander[...] = hit.astype(BF16)

    def expand(columns, c, lb):
        return jnp.dot(
            columns, expander[:, c * width + lb : c * width + lb + lanes], preferred_element_type=F32
        )

    for copy in small[1:]:
        copy.wait()
    skip_columns = split_columns(turn_row(skip[...]))
    for lb in range(0, channels, lanes):
        skip_row[:, lb : lb + lanes] = expand(skip_columns[0:16, :], 0, lb)[0:8]
    rate = jnp.exp(turn_row(decay[...]))

    def tail_before(rows):
        return jnp.where(mine > 0, rows.astype(F32), 0.0)

    def signal_of(k, c, before):
        for lb in range(0, width, lanes):
            here = slice(lb, lb + lanes)
            taps = conv_v[:, pl.ds(pl.multiple_of(me * channels + c * width + lb, lanes), lanes)]
            signal[k, c, :, here] = convolved(
                raw_v[k, c, :, here].astype(F32), before(here), taps.astype(F32)
            )

    def factors_of(k, before):
        for part_index, target in ((0, b_rows), (1, c_rows)):
            taps = conv_f[:, me, part_index, :].astype(F32)
            target[k] = convolved(raw_f[k, :, part_index, :].astype(F32), before(part_index), taps)

    @pl.loop(1, GROUPS)
    def _(j):
        stp_arrive(other(j)).wait_recv()

    steps = softplus_below_zero(stp_recv[...].astype(F32))
    step_t[...] = steps
    falls = (steps * rate[None]).reshape(GROUPS * heads, SPAN)
    upto = (
        lax.broadcasted_iota(jnp.int32, (SPAN, SPAN), 0)
        <= lax.broadcasted_iota(jnp.int32, (SPAN, SPAN), 1)
    ).astype(F32)
    run_t[...] = -jnp.dot(
        falls, upto, preferred_element_type=F32, precision=lax.Precision.HIGHEST
    ).reshape(GROUPS, heads, SPAN)

    def columns_of(k, prior):
        running = run_t[k]
        ending = running[:, SPAN - 1 : SPAN]
        w_s[k] = split_columns(jnp.exp(ending - running) * step_t[k])
        t_s[k] = split_columns(jnp.exp(running))
        g_s[k] = split_columns(jnp.exp(running + prior))
        run_c[k] = jnp.transpose(
            jnp.concatenate([running, jnp.zeros((128 - heads, SPAN), F32)], axis=0)
        )
        return prior + ending

    lax.fori_loop(0, GROUPS, columns_of, jnp.zeros((heads, 1), F32))

    @pl.loop(1, supers)
    def _(j):
        d_out(other_super(j)).start()

    d_recv[mine] = g_s[GROUPS - 1, SPAN - 16 : SPAN, :]

    @pl.loop(1, GROUPS)
    def _(j):
        fac_arrive(other(j)).wait_recv()

    own_factors.wait()
    tail_f_copy.start()

    causal = lax.broadcasted_iota(jnp.int32, (SPAN, SPAN), 0) >= lax.broadcasted_iota(
        jnp.int32, (SPAN, SPAN), 1
    )

    def scores_of(k):
        turned = jnp.transpose(b_rows[k].astype(F32)).astype(BF16)
        b_t[k] = turned
        scores[k] = jnp.where(causal, jnp.dot(c_rows[k], turned, preferred_element_type=F32), 0.0)

    @pl.loop(1, GROUPS)
    def _(k):
        factors_of(k, lambda i: raw_f[k - 1, SPAN - 8 : SPAN, i, :].astype(F32))
        scores_of(k)

    tail_f_copy.wait_recv()
    factors_of(0, lambda i: tail_before(tail_f[:, i, :])[8:16])
    scores_of(0)

    def wait_chunk(c):
        @pl.loop(1, GROUPS)
        def _(j):
            sig_out(other(j), c).wait_send()
            if c + AHEAD < CHUNKS:
                sig_out(other(j), c + AHEAD).start()

        @pl.loop(1, GROUPS)
        def _(j):
            sig_in(other(j), c).wait_recv()

        own_copy(c).wait()
        tail_v_copy(c).start()

        @pl.loop(1, GROUPS)
        def _(k):
            signal_of(k, c, lambda here: raw_v[k - 1, c, SPAN - 16 : SPAN, here].astype(F32)[8:16])

        tail_v_copy(c).wait_recv()
        signal_of(0, c, lambda here: tail_before(tail_v[c, :, here])[8:16])

    def accumulate(c):
        state[...] = jnp.zeros_like(state)

        @pl.loop(0, GROUPS)
        def _(k):
            for lb in range(0, width, lanes):
                here = slice(lb, lb + lanes)
                weight = expand(w_s[k], c, lb)
                weighted[:, here] = (weight * signal[k, c, :, here].astype(F32)).astype(BF16)
                ending = expand(t_s[k, SPAN - 16 : SPAN, :], c, lb)[15:16]
                held = state[:, here]
                local_entry[k, :, here] = held.astype(BF16)
                state[:, here] = held * ending + jnp.dot(
                    b_t[k], weighted[:, here], preferred_element_type=F32
                )

        s_send[c] = state[...].astype(BF16)

        @pl.loop(1, supers)
        def _(j):
            st_out(other_super(j), c).start()

        st_recv[c, mine] = s_send[c, part_of(mine), :]

    def inside(c):
        low_half = lax.broadcasted_iota(jnp.int32, (SPAN, 128), 1) < HEAD_DIM

        @pl.loop(0, GROUPS)
        def _(k):
            for pair in range(chunk_heads // 2):
                here = slice(pair * 128, pair * 128 + 128)
                there = slice(c * width + pair * 128, c * width + pair * 128 + 128)
                mixes = []
                for h in (c * chunk_heads + 2 * pair, c * chunk_heads + 2 * pair + 1):
                    gap = run_c[k, :, h : h + 1] - run_t[k, h : h + 1, :]
                    mixes.append(
                        (jnp.exp(jnp.minimum(gap, 0.0)) * step_t[k, h : h + 1, :] * scores[k]).astype(BF16)
                    )
                values = signal[k, c, :, here].astype(F32)
                both = jnp.concatenate(
                    [
                        jnp.where(low_half, values, 0.0).astype(BF16),
                        jnp.where(low_half, 0.0, values).astype(BF16),
                    ],
                    axis=0,
                )
                part[k, :, there] = (
                    jnp.dot(jnp.concatenate(mixes, axis=1), both, preferred_element_type=F32)
                    + skip_row[0:1, there] * values
                )
            for lb in range(0, width, lanes):
                there = slice(c * width + lb, c * width + lb + lanes)
                held = jnp.dot(
                    c_rows[k], local_entry[k, :, lb : lb + lanes], preferred_element_type=F32
                )
                part[k, :, there] = part[k, :, there] + expand(t_s[k], c, lb) * held

    def exchange(c):
        if c == 0:

            @pl.loop(1, supers)
            def _(j):
                d_arrive(other_super(j)).wait_recv()

            for j in range(supers):
                d_wide[j : j + 1, :] = jnp.dot(
                    d_recv[j], expander[...], preferred_element_type=F32
                )[15:16]

        @pl.loop(1, supers)
        def _(j):
            st_arrive(other_super(j), c).wait_recv()

        entry = jnp.zeros((slice_rows, width), F32)
        for j in range(supers):
            e_send[c, j] = entry.astype(BF16)
            if j + 1 < supers:
                entry = entry * d_wide[j : j + 1, c * width : (c + 1) * width] + st_recv[c, j].astype(F32)

        @pl.loop(1, supers)
        def _(j):
            e_out(other_super(j), c).start()

        e_recv[c, part_of(mine), :] = e_send[c, mine]

    def results(c):
        @pl.loop(1, supers)
        def _(j):
            e_arrive(other_super(j), c).wait_recv()

        def result_of(k, target):
            for lb in range(0, width, lanes):
                there = slice(c * width + lb, c * width + lb + lanes)
                held = jnp.dot(
                    c_rows[k], e_recv[c, :, lb : lb + lanes], preferred_element_type=F32
                )
                target[:, lb : lb + lanes] = (
                    part[k, :, there] + expand(g_s[k], c, lb) * held
                ).astype(BF16)

        @pl.loop(1, GROUPS)
        def _(j):
            k = other(j)
            result_of(k, y_send.at[k, c])
            y_out(k, c).start()

        result_of(me, y_recv.at[me, c])

    def out_copy(k):
        columns = pl.ds(pl.multiple_of(k * channels, channels), channels)
        return pltpu.make_async_copy(out.at[:, columns], out_hbm.at[:, columns], out_sem.at[k])

    def finish(c):
        if c == 0:
            gate_copy.wait()

        @pl.loop(0, GROUPS)
        def _(j):
            k = other(GROUPS - j)

            @pl.when(j > 0)
            def _():
                y_arrive(k, c).wait_recv()

            total = jnp.zeros((SPAN, 128), F32)
            if c > 0:
                total = squares[k]
            for lb in range(0, width, lanes):
                here = pl.ds(pl.multiple_of(k * channels + c * width + lb, lanes), lanes)
                value = y_recv[k, c, :, lb : lb + lanes].astype(F32) * silu_wide(
                    gate[:, here].astype(F32)
                )
                gated[k, :, c * width + lb : c * width + lb + lanes] = value
                square = value * value
                for start in range(0, lanes, 128):
                    total = total + square[:, start : start + 128]
            if c + 1 < CHUNKS:
                squares[k] = total
            else:
                mean = jnp.sum(total, axis=1, keepdims=True) * (1.0 / channels)
                inverse = lax.rsqrt(mean + 1e-05)
                for lb in range(0, channels, LANES):
                    here = pl.ds(pl.multiple_of(k * channels + lb, LANES), LANES)
                    out[:, here] = (
                        gated[k, :, lb : lb + LANES] * inverse * gain[k, :, lb : lb + LANES]
                    ).astype(BF16)
                out_copy(k).start()

    wait_chunk(0)
    accumulate(0)
    inside(0)
    exchange(0)
    for c in range(1, CHUNKS):
        wait_chunk(c)
        accumulate(c)
        results(c - 1)
        inside(c)
        exchange(c)
    results(CHUNKS - 1)
    for c in range(CHUNKS):
        finish(c)

    tail_f_copy.wait_send()
    for c in range(CHUNKS):
        tail_v_copy(c).wait_send()

    @pl.loop(1, GROUPS)
    def _(j):
        g = other(j)
        stp_out(g).wait_send()
        fac_out(g).wait_send()
        for c in range(CHUNKS):
            y_out(g, c).wait_send()

    @pl.loop(1, supers)
    def _(j):
        peer = other_super(j)
        d_out(peer).wait_send()
        for c in range(CHUNKS):
            st_out(peer, c).wait_send()
            e_out(peer, c).wait_send()

    @pl.loop(0, GROUPS)
    def _(j):
        out_copy(other(j)).wait()


def move(strips, source, target, held, in_sem, out_sem):
    high = held.shape[0] // strips
    reads, writes = [], []
    for i in range(strips):
        here = pl.ds(i * high, high)
        reads.append(pltpu.make_async_copy(source.at[here], held.at[here], in_sem.at[i]))
        writes.append(pltpu.make_async_copy(held.at[here], target.at[here], out_sem.at[i]))
    for read in reads:
        read.start()
    for read, write in zip(reads, writes):
        read.wait()
        write.start()
    for write in writes:
        write.wait()


def local(
    values_in, factors_in, step_raw, gate_in, conv_values, conv_factors, decay_log, skip_gain, norm_gain
):
    rows, inner = values_in.shape
    heads = step_raw.shape[1] // GROUPS
    channels = heads * HEAD_DIM
    width = channels // CHUNKS
    supers = lax.axis_size("seq") // 2
    slice_rows = STATE // supers

    gain = norm_gain.reshape(GROUPS, 1, channels)

    hbm = pl.BlockSpec(memory_space=pl.ANY)
    dma = pltpu.SemaphoreType.DMA
    small = [step_raw, conv_values, conv_factors, decay_log.reshape(1, -1), skip_gain.reshape(1, -1), gain]
    scratch = [pltpu.VMEM(array.shape, array.dtype) for array in small] + [
        pltpu.VMEM((SPAN, inner), BF16),
        pltpu.VMEM((SPAN, inner), BF16),
        pltpu.VMEM((CHUNKS, 16, width), BF16),
        pltpu.VMEM((16, 2, STATE), BF16),
        pltpu.VMEM((GROUPS, CHUNKS, SPAN, width), BF16),
        pltpu.VMEM((GROUPS, SPAN, 2, STATE), BF16),
        pltpu.VMEM((GROUPS, CHUNKS, SPAN, width), BF16),
        pltpu.VMEM((GROUPS, SPAN, STATE), BF16),
        pltpu.VMEM((GROUPS, SPAN, STATE), BF16),
        pltpu.VMEM((GROUPS, heads, SPAN), BF16),
        pltpu.VMEM((GROUPS, heads, SPAN), BF16),
        pltpu.VMEM((GROUPS * heads, 128), F32),
        pltpu.VMEM((8, channels), F32),
        pltpu.VMEM((GROUPS, heads, SPAN), F32),
        pltpu.VMEM((GROUPS, heads, SPAN), F32),
        pltpu.VMEM((GROUPS, SPAN, 128), F32),
        pltpu.VMEM((GROUPS, SPAN, 128), BF16),
        pltpu.VMEM((GROUPS, SPAN, 128), BF16),
        pltpu.VMEM((GROUPS, SPAN, 128), BF16),
        pltpu.VMEM((GROUPS, STATE, SPAN), BF16),
        pltpu.VMEM((GROUPS, SPAN, SPAN), F32),
        pltpu.VMEM((128, channels), BF16),
        pltpu.VMEM((STATE, width), F32),
        pltpu.VMEM((GROUPS, STATE, width), BF16),
        pltpu.VMEM((CHUNKS, STATE, width), BF16),
        pltpu.VMEM((CHUNKS, supers, slice_rows, width), BF16),
        pltpu.VMEM((CHUNKS, supers, slice_rows, width), BF16),
        pltpu.VMEM((CHUNKS, STATE, width), BF16),
        pltpu.VMEM((supers, 16, 128), BF16),
        pltpu.VMEM((max(supers, 8), channels), F32),
        pltpu.VMEM((GROUPS, SPAN, channels), F32),
        pltpu.VMEM((SPAN, width), BF16),
        pltpu.VMEM((GROUPS, SPAN, channels), F32),
        pltpu.VMEM((GROUPS, SPAN, 128), F32),
        pltpu.VMEM((GROUPS, CHUNKS, SPAN, width), BF16),
        pltpu.VMEM((GROUPS, CHUNKS, SPAN, width), BF16),
        dma((CHUNKS + 1,)), dma, dma((GROUPS,)), dma((CHUNKS + 1,)), dma((CHUNKS + 1,)),
        dma((GROUPS, CHUNKS)), dma((GROUPS, CHUNKS)),
        dma((GROUPS,)), dma((GROUPS,)),
        dma((GROUPS,)), dma((GROUPS,)),
        dma((supers,)), dma((supers,)),
        dma((CHUNKS, supers)), dma((CHUNKS, supers)),
        dma((CHUNKS, supers)), dma((CHUNKS, supers)),
        dma((GROUPS, CHUNKS)), dma((GROUPS, CHUNKS)),
        pltpu.SemaphoreType.REGULAR((supers.bit_length() - 1,)), dma((6,)),
    ]
    mixed = pl.pallas_call(
        partial(body, heads=heads, supers=supers),
        out_shape=jax.ShapeDtypeStruct((rows, inner), BF16),
        in_specs=[hbm] * 9,
        out_specs=hbm,
        scratch_shapes=scratch,
        compiler_params=pltpu.CompilerParams(
            collective_id=0, has_side_effects=True, vmem_limit_bytes=61 * 2**20
        ),
        name="layer",
    )(
        values_in, gate_in, factors_in, *small
    )
    strips = 4
    return pl.pallas_call(
        partial(move, strips),
        out_shape=jax.ShapeDtypeStruct((rows, inner), BF16),
        in_specs=[hbm],
        out_specs=hbm,
        scratch_shapes=[pltpu.VMEM((rows, inner), BF16), dma((strips,)), dma((strips,))],
        name="move",
    )(mixed)


def solution(mesh):
    rows = P(("seq", "head"), None)
    placed = (rows, P(("seq", "head"), None, None, None), rows, rows, P(), P(), P(), P(), P())
    return jax.shard_map(local, mesh=mesh, in_specs=placed, out_specs=rows, check_vma=False)
```

```python
from functools import partial

import jax
import jax.numpy as jnp
from jax import lax
from jax.experimental import pallas as pl
from jax.experimental.pallas import tpu as pltpu
from jax.sharding import PartitionSpec as P

HEAD_DIM = 64
STATE = 256
GROUPS = 8
SPAN = 128
CONV = 4
CHUNKS = 4
AHEAD = 4
LANES = 256
F32 = jnp.float32
BF16 = jnp.bfloat16
MESH = pl.DeviceIdType.MESH


def silu(value):
    return value * pl.reciprocal(1.0 + jnp.exp(-value))


def silu_wide(value):
    inner = value * pl.reciprocal(1.0 + jnp.exp(jnp.minimum(-value, 87.0)))
    return jnp.where(value < -87.0, 0.0, inner)


def softplus_below_zero(value):
    e = jnp.exp(value)
    z = e / (2.0 + e)
    q = z * z
    series = 1.0 / 15.0
    for odd in (13.0, 11.0, 9.0, 7.0, 5.0, 3.0, 1.0):
        series = series * q + 1.0 / odd
    return 2.0 * z * series


def split_columns(rows):
    heads = rows.shape[0]
    high = rows.astype(BF16).astype(F32)
    middle = (rows - high).astype(BF16).astype(F32)
    low = rows - high - middle
    parts = [high, middle, low]
    if 128 > 3 * heads:
        parts.append(jnp.zeros((128 - 3 * heads, rows.shape[1]), F32))
    return jnp.transpose(jnp.concatenate(parts, axis=0)).astype(BF16)


def convolved(current, before, taps):
    padded = jnp.concatenate([before, current], axis=0)
    total = padded[5 : 5 + SPAN] * taps[0:1]
    for offset in range(1, CONV):
        total = total + padded[5 + offset : 5 + offset + SPAN] * taps[offset : offset + 1]
    return silu(total).astype(BF16)


def body(
    values_hbm, gate_hbm, fac_hbm, step_hbm, conv_v_hbm, conv_f_hbm, decay_hbm, skip_hbm, gain_hbm,
    out_hbm,
    step_in, conv_v, conv_f, decay, skip, gain, out, gate, tail_v, tail_f, raw_v, raw_f, signal, b_rows, c_rows, stp_send, stp_recv,
    head_col, skip_row, step_t, run_t, run_c, w_s, t_s, g_s, b_t, scores, expander,
    state, local_entry, s_send, st_recv, e_send, e_recv, d_recv, d_wide,
    part, weighted, gated, squares, y_send, y_recv,
    own_sem, gate_sem, out_sem, tail_ss, tail_rs,
    sig_ss, sig_rs, fac_ss, fac_rs, stp_ss, stp_rs, d_ss, d_rs,
    st_ss, st_rs, e_ss, e_rs, y_ss, y_rs, met, all_met, small_sem,
    *, heads, supers,
):
    channels = heads * HEAD_DIM
    width = channels // CHUNKS
    chunk_heads = heads // CHUNKS
    slice_rows = STATE // supers
    lanes = min(LANES, width)

    seq, col = lax.axis_index("seq"), lax.axis_index("head")
    core = lax.rem(seq, 2)
    mine = seq // 2
    me = core * 4 + col
    place = mine * GROUPS + me

    def owner(k):
        return (mine * 2 + k // 4, lax.rem(k, 4))

    def column(j):
        return (j * 2 + core, col)

    def anywhere(index):
        k = lax.rem(index, GROUPS)
        return ((index // GROUPS) * 2 + k // 4, lax.rem(k, 4))

    def other(j):
        return lax.rem(me + j, GROUPS)

    def other_super(j):
        return lax.rem(mine + j, supers)

    following = column(other_super(1))
    previous = column(other_super(supers - 1))

    def columns_of_chunk(g, c):
        return pl.ds(pl.multiple_of(g * channels + c * width, width), width)

    def own_copy(c):
        return pltpu.make_async_copy(
            values_hbm.at[:, columns_of_chunk(me, c)], raw_v.at[me, c], own_sem.at[c]
        )

    own_factors = pltpu.make_async_copy(fac_hbm.at[:, me], raw_f.at[me], own_sem.at[CHUNKS])
    gate_copy = pltpu.make_async_copy(gate_hbm, gate, gate_sem)

    def remote(src, dst, ss, rs, device):
        return pltpu.make_async_remote_copy(
            src_ref=src, dst_ref=dst, send_sem=ss, recv_sem=rs, device_id=device, device_id_type=MESH
        )

    def sig_out(g, c):
        return remote(
            values_hbm.at[:, columns_of_chunk(g, c)], raw_v.at[me, c], sig_ss.at[g, c], sig_rs.at[me, c], owner(g)
        )

    def sig_in(k, c):
        return remote(
            values_hbm.at[:, columns_of_chunk(k, c)], raw_v.at[k, c], sig_ss.at[k, c], sig_rs.at[k, c], owner(k)
        )

    def fac_out(g):
        return remote(fac_hbm.at[:, g], raw_f.at[me], fac_ss.at[g], fac_rs.at[me], owner(g))

    def fac_arrive(k):
        return remote(fac_hbm.at[:, k], raw_f.at[k], fac_ss.at[k], fac_rs.at[k], owner(k))

    last_rows = pl.ds(SPAN - 16, 16)

    def tail_v_copy(c):
        return remote(
            raw_v.at[GROUPS - 1, c, last_rows], tail_v.at[c], tail_ss.at[c], tail_rs.at[c], following
        )

    tail_f_copy = remote(
        raw_f.at[GROUPS - 1, last_rows], tail_f, tail_ss.at[CHUNKS], tail_rs.at[CHUNKS], following
    )

    def stp_out(g):
        return remote(stp_send.at[g], stp_recv.at[me], stp_ss.at[g], stp_rs.at[me], owner(g))

    def stp_arrive(k):
        return remote(stp_send.at[k], stp_recv.at[k], stp_ss.at[k], stp_rs.at[k], owner(k))

    def d_out(j):
        return remote(
            g_s.at[GROUPS - 1, pl.ds(SPAN - 16, 16)], d_recv.at[mine], d_ss.at[j], d_rs.at[mine], column(j)
        )

    def d_arrive(j):
        return remote(
            g_s.at[GROUPS - 1, pl.ds(SPAN - 16, 16)], d_recv.at[j], d_ss.at[j], d_rs.at[j], column(j)
        )

    def part_of(j):
        return pl.ds(pl.multiple_of(j * slice_rows, slice_rows), slice_rows)

    def st_out(j, c):
        return remote(
            s_send.at[c, part_of(j)], st_recv.at[c, mine], st_ss.at[c, j], st_rs.at[c, mine], column(j)
        )

    def st_arrive(j, c):
        return remote(s_send.at[c, part_of(j)], st_recv.at[c, j], st_ss.at[c, j], st_rs.at[c, j], column(j))

    def e_out(j, c):
        return remote(
            e_send.at[c, j], e_recv.at[c, part_of(mine)], e_ss.at[c, j], e_rs.at[c, mine], column(j)
        )

    def e_arrive(j, c):
        return remote(e_send.at[c, j], e_recv.at[c, part_of(j)], e_ss.at[c, j], e_rs.at[c, j], column(j))

    def y_out(k, c):
        return remote(y_send.at[k, c], y_recv.at[me, c], y_ss.at[k, c], y_rs.at[me, c], owner(k))

    def y_arrive(k, c):
        return remote(y_send.at[k, c], y_recv.at[k, c], y_ss.at[k, c], y_rs.at[k, c], owner(k))

    small = [
        pltpu.make_async_copy(source, target, small_sem.at[i])
        for i, (source, target) in enumerate(
            [
                (step_hbm, step_in), (conv_v_hbm, conv_v), (conv_f_hbm, conv_f),
                (decay_hbm, decay), (skip_hbm, skip), (gain_hbm, gain),
            ]
        )
    ]
    small[0].start()
    barrier = pltpu.get_barrier_semaphore()

    @pl.loop(1, GROUPS)
    def _(j):
        pl.semaphore_signal(barrier, inc=1, device_id=owner(other(j)), device_id_type=MESH)

    pairs = [1 << d for d in range(supers.bit_length() - 1)]

    def opposite(pair):
        return column(mine + pair - 2 * pair * lax.rem(mine // pair, 2))

    @pl.when(me == 0)
    def _():
        for pair in pairs:
            pl.semaphore_signal(barrier, inc=1, device_id=opposite(pair), device_id_type=MESH)

    small[0].wait()
    for start in range(0, GROUPS * heads, 128):
        count = min(128, GROUPS * heads - start)
        turned = jnp.transpose(step_in[:, start : start + count].astype(F32)).astype(BF16)
        stp_send[start // heads : (start + count) // heads] = turned.reshape(count // heads, heads, SPAN)

    pl.semaphore_wait(barrier, GROUPS - 1 + jnp.where(me == 0, len(pairs), 0))

    @pl.loop(1, GROUPS)
    def _(j):
        stp_out(other(j)).start()

    @pl.loop(1, GROUPS)
    def _(j):
        fac_out(other(j)).start()

    for c in range(AHEAD):

        @pl.loop(1, GROUPS)
        def _(j):
            sig_out(other(j), c).start()

    own_factors.start()
    for copy in small[1:]:
        copy.start()
    for c in range(CHUNKS):
        own_copy(c).start()
    gate_copy.start()

    stp_recv[me] = stp_send[me]

    def turn_row(row):
        for start in range(0, GROUPS * heads, 128):
            count = min(128, GROUPS * heads - start)
            head_col[start : start + count, :] = jnp.transpose(
                jnp.broadcast_to(row[:, start : start + count], (128, count))
            )
        return head_col[pl.ds(pl.multiple_of(me * heads, heads), heads), :]

    @pl.when(me == 0)
    def _():
        for d, pair in enumerate(pairs):
            pl.semaphore_signal(met.at[d], inc=1, device_id=opposite(pair), device_id_type=MESH)
            pl.semaphore_wait(met.at[d], 1)

        @pl.loop(1, GROUPS)
        def _(j):
            pl.semaphore_signal(all_met, inc=1, device_id=owner(other(j)), device_id_type=MESH)

    slot = lax.broadcasted_iota(jnp.int32, (128, channels), 0)
    channel = lax.broadcasted_iota(jnp.int32, (128, channels), 1)
    hit = jnp.zeros((128, channels), F32)
    for piece in range(3):
        hit = jnp.where(slot == channel // HEAD_DIM + piece * heads, 1.0, hit)
    expander[...] = hit.astype(BF16)

    def expand(columns, c, lb):
        return jnp.dot(
            columns, expander[:, c * width + lb : c * width + lb + lanes], preferred_element_type=F32
        )

    for copy in small[1:]:
        copy.wait()
    skip_columns = split_columns(turn_row(skip[...]))
    for lb in range(0, channels, lanes):
        skip_row[:, lb : lb + lanes] = expand(skip_columns[0:16, :], 0, lb)[0:8]
    rate = jnp.exp(turn_row(decay[...]))

    def tail_before(rows):
        return jnp.where(mine > 0, rows.astype(F32), 0.0)

    def signal_of(k, c, before):
        for lb in range(0, width, lanes):
            here = slice(lb, lb + lanes)
            taps = conv_v[:, pl.ds(pl.multiple_of(me * channels + c * width + lb, lanes), lanes)]
            signal[k, c, :, here] = convolved(
                raw_v[k, c, :, here].astype(F32), before(here), taps.astype(F32)
            )

    def factors_of(k, before):
        for part_index, target in ((0, b_rows), (1, c_rows)):
            taps = conv_f[:, me, part_index, :].astype(F32)
            target[k] = convolved(raw_f[k, :, part_index, :].astype(F32), before(part_index), taps)

    @pl.loop(1, GROUPS)
    def _(j):
        stp_arrive(other(j)).wait_recv()

    steps = softplus_below_zero(stp_recv[...].astype(F32))
    step_t[...] = steps
    falls = (steps * rate[None]).reshape(GROUPS * heads, SPAN)
    upto = (
        lax.broadcasted_iota(jnp.int32, (SPAN, SPAN), 0)
        <= lax.broadcasted_iota(jnp.int32, (SPAN, SPAN), 1)
    ).astype(F32)
    run_t[...] = -jnp.dot(
        falls, upto, preferred_element_type=F32, precision=lax.Precision.HIGHEST
    ).reshape(GROUPS, heads, SPAN)

    def columns_of(k, prior):
        running = run_t[k]
        ending = running[:, SPAN - 1 : SPAN]
        w_s[k] = split_columns(jnp.exp(ending - running) * step_t[k])
        t_s[k] = split_columns(jnp.exp(running))
        g_s[k] = split_columns(jnp.exp(running + prior))
        run_c[k] = jnp.transpose(
            jnp.concatenate([running, jnp.zeros((128 - heads, SPAN), F32)], axis=0)
        )
        return prior + ending

    lax.fori_loop(0, GROUPS, columns_of, jnp.zeros((heads, 1), F32))

    @pl.when(me != 0)
    def _():
        pl.semaphore_wait(all_met, 1)

    @pl.loop(1, supers)
    def _(j):
        d_out(other_super(j)).start()

    d_recv[mine] = g_s[GROUPS - 1, SPAN - 16 : SPAN, :]

    @pl.loop(1, GROUPS)
    def _(j):
        fac_arrive(other(j)).wait_recv()

    own_factors.wait()
    tail_f_copy.start()

    causal = lax.broadcasted_iota(jnp.int32, (SPAN, SPAN), 0) >= lax.broadcasted_iota(
        jnp.int32, (SPAN, SPAN), 1
    )

    def scores_of(k):
        turned = jnp.transpose(b_rows[k].astype(F32)).astype(BF16)
        b_t[k] = turned
        scores[k] = jnp.where(causal, jnp.dot(c_rows[k], turned, preferred_element_type=F32), 0.0)

    @pl.loop(1, GROUPS)
    def _(k):
        factors_of(k, lambda i: raw_f[k - 1, SPAN - 8 : SPAN, i, :].astype(F32))
        scores_of(k)

    tail_f_copy.wait_recv()
    factors_of(0, lambda i: tail_before(tail_f[:, i, :])[8:16])
    scores_of(0)

    def wait_chunk(c):
        @pl.loop(1, GROUPS)
        def _(j):
            sig_out(other(j), c).wait_send()
            if c + AHEAD < CHUNKS:
                sig_out(other(j), c + AHEAD).start()

        @pl.loop(1, GROUPS)
        def _(j):
            sig_in(other(j), c).wait_recv()

        own_copy(c).wait()
        tail_v_copy(c).start()

        @pl.loop(1, GROUPS)
        def _(k):
            signal_of(k, c, lambda here: raw_v[k - 1, c, SPAN - 16 : SPAN, here].astype(F32)[8:16])

        tail_v_copy(c).wait_recv()
        signal_of(0, c, lambda here: tail_before(tail_v[c, :, here])[8:16])

    def accumulate(c):
        state[...] = jnp.zeros_like(state)

        @pl.loop(0, GROUPS)
        def _(k):
            for lb in range(0, width, lanes):
                here = slice(lb, lb + lanes)
                weight = expand(w_s[k], c, lb)
                weighted[:, here] = (weight * signal[k, c, :, here].astype(F32)).astype(BF16)
                ending = expand(t_s[k, SPAN - 16 : SPAN, :], c, lb)[15:16]
                held = state[:, here]
                local_entry[k, :, here] = held.astype(BF16)
                state[:, here] = held * ending + jnp.dot(
                    b_t[k], weighted[:, here], preferred_element_type=F32
                )

        s_send[c] = state[...].astype(BF16)

        @pl.loop(1, supers)
        def _(j):
            st_out(other_super(j), c).start()

        st_recv[c, mine] = s_send[c, part_of(mine), :]

    def inside(c):
        low_half = lax.broadcasted_iota(jnp.int32, (SPAN, 128), 1) < HEAD_DIM

        @pl.loop(0, GROUPS)
        def _(k):
            for pair in range(chunk_heads // 2):
                here = slice(pair * 128, pair * 128 + 128)
                there = slice(c * width + pair * 128, c * width + pair * 128 + 128)
                mixes = []
                for h in (c * chunk_heads + 2 * pair, c * chunk_heads + 2 * pair + 1):
                    gap = run_c[k, :, h : h + 1] - run_t[k, h : h + 1, :]
                    mixes.append(
                        (jnp.exp(jnp.minimum(gap, 0.0)) * step_t[k, h : h + 1, :] * scores[k]).astype(BF16)
                    )
                values = signal[k, c, :, here].astype(F32)
                both = jnp.concatenate(
                    [
                        jnp.where(low_half, values, 0.0).astype(BF16),
                        jnp.where(low_half, 0.0, values).astype(BF16),
                    ],
                    axis=0,
                )
                part[k, :, there] = (
                    jnp.dot(jnp.concatenate(mixes, axis=1), both, preferred_element_type=F32)
                    + skip_row[0:1, there] * values
                )
            for lb in range(0, width, lanes):
                there = slice(c * width + lb, c * width + lb + lanes)
                held = jnp.dot(
                    c_rows[k], local_entry[k, :, lb : lb + lanes], preferred_element_type=F32
                )
                part[k, :, there] = part[k, :, there] + expand(t_s[k], c, lb) * held

    def exchange(c):
        if c == 0:

            @pl.loop(1, supers)
            def _(j):
                d_arrive(other_super(j)).wait_recv()

            for j in range(supers):
                d_wide[j : j + 1, :] = jnp.dot(
                    d_recv[j], expander[...], preferred_element_type=F32
                )[15:16]

        @pl.loop(1, supers)
        def _(j):
            st_arrive(other_super(j), c).wait_recv()

        entry = jnp.zeros((slice_rows, width), F32)
        for j in range(supers):
            e_send[c, j] = entry.astype(BF16)
            if j + 1 < supers:
                entry = entry * d_wide[j : j + 1, c * width : (c + 1) * width] + st_recv[c, j].astype(F32)

        @pl.loop(1, supers)
        def _(j):
            e_out(other_super(j), c).start()

        e_recv[c, part_of(mine), :] = e_send[c, mine]

    def results(c):
        @pl.loop(1, supers)
        def _(j):
            e_arrive(other_super(j), c).wait_recv()

        def result_of(k, target):
            for lb in range(0, width, lanes):
                there = slice(c * width + lb, c * width + lb + lanes)
                held = jnp.dot(
                    c_rows[k], e_recv[c, :, lb : lb + lanes], preferred_element_type=F32
                )
                target[:, lb : lb + lanes] = (
                    part[k, :, there] + expand(g_s[k], c, lb) * held
                ).astype(BF16)

        @pl.loop(1, GROUPS)
        def _(j):
            k = other(j)
            result_of(k, y_send.at[k, c])
            y_out(k, c).start()

        result_of(me, y_recv.at[me, c])

    def out_copy(k):
        columns = pl.ds(pl.multiple_of(k * channels, channels), channels)
        return pltpu.make_async_copy(out.at[:, columns], out_hbm.at[:, columns], out_sem.at[k])

    def finish(c):
        if c == 0:
            gate_copy.wait()

        @pl.loop(0, GROUPS)
        def _(j):
            k = other(GROUPS - j)

            @pl.when(j > 0)
            def _():
                y_arrive(k, c).wait_recv()

            total = jnp.zeros((SPAN, 128), F32)
            if c > 0:
                total = squares[k]
            for lb in range(0, width, lanes):
                here = pl.ds(pl.multiple_of(k * channels + c * width + lb, lanes), lanes)
                value = y_recv[k, c, :, lb : lb + lanes].astype(F32) * silu_wide(
                    gate[:, here].astype(F32)
                )
                gated[k, :, c * width + lb : c * width + lb + lanes] = value
                square = value * value
                for start in range(0, lanes, 128):
                    total = total + square[:, start : start + 128]
            if c + 1 < CHUNKS:
                squares[k] = total
            else:
                mean = jnp.sum(total, axis=1, keepdims=True) * (1.0 / channels)
                inverse = lax.rsqrt(mean + 1e-05)
                for lb in range(0, channels, LANES):
                    here = pl.ds(pl.multiple_of(k * channels + lb, LANES), LANES)
                    out[:, here] = (
                        gated[k, :, lb : lb + LANES] * inverse * gain[k, :, lb : lb + LANES]
                    ).astype(BF16)
                out_copy(k).start()

    wait_chunk(0)
    accumulate(0)
    inside(0)
    exchange(0)
    for c in range(1, CHUNKS):
        wait_chunk(c)
        accumulate(c)
        results(c - 1)
        inside(c)
        exchange(c)
    results(CHUNKS - 1)
    for c in range(CHUNKS):
        finish(c)

    tail_f_copy.wait_send()
    for c in range(CHUNKS):
        tail_v_copy(c).wait_send()

    @pl.loop(1, GROUPS)
    def _(j):
        g = other(j)
        stp_out(g).wait_send()
        fac_out(g).wait_send()
        for c in range(CHUNKS):
            y_out(g, c).wait_send()

    @pl.loop(1, supers)
    def _(j):
        peer = other_super(j)
        d_out(peer).wait_send()
        for c in range(CHUNKS):
            st_out(peer, c).wait_send()
            e_out(peer, c).wait_send()

    @pl.loop(0, GROUPS)
    def _(j):
        out_copy(other(j)).wait()


def move(strips, source, target, held, in_sem, out_sem):
    high = held.shape[0] // strips
    reads, writes = [], []
    for i in range(strips):
        here = pl.ds(i * high, high)
        reads.append(pltpu.make_async_copy(source.at[here], held.at[here], in_sem.at[i]))
        writes.append(pltpu.make_async_copy(held.at[here], target.at[here], out_sem.at[i]))
    for read in reads:
        read.start()
    for read, write in zip(reads, writes):
        read.wait()
        write.start()
    for write in writes:
        write.wait()


def local(
    values_in, factors_in, step_raw, gate_in, conv_values, conv_factors, decay_log, skip_gain, norm_gain
):
    rows, inner = values_in.shape
    heads = step_raw.shape[1] // GROUPS
    channels = heads * HEAD_DIM
    width = channels // CHUNKS
    supers = lax.axis_size("seq") // 2
    slice_rows = STATE // supers

    gain = norm_gain.reshape(GROUPS, 1, channels)

    hbm = pl.BlockSpec(memory_space=pl.ANY)
    dma = pltpu.SemaphoreType.DMA
    small = [step_raw, conv_values, conv_factors, decay_log.reshape(1, -1), skip_gain.reshape(1, -1), gain]
    scratch = [pltpu.VMEM(array.shape, array.dtype) for array in small] + [
        pltpu.VMEM((SPAN, inner), BF16),
        pltpu.VMEM((SPAN, inner), BF16),
        pltpu.VMEM((CHUNKS, 16, width), BF16),
        pltpu.VMEM((16, 2, STATE), BF16),
        pltpu.VMEM((GROUPS, CHUNKS, SPAN, width), BF16),
        pltpu.VMEM((GROUPS, SPAN, 2, STATE), BF16),
        pltpu.VMEM((GROUPS, CHUNKS, SPAN, width), BF16),
        pltpu.VMEM((GROUPS, SPAN, STATE), BF16),
        pltpu.VMEM((GROUPS, SPAN, STATE), BF16),
        pltpu.VMEM((GROUPS, heads, SPAN), BF16),
        pltpu.VMEM((GROUPS, heads, SPAN), BF16),
        pltpu.VMEM((GROUPS * heads, 128), F32),
        pltpu.VMEM((8, channels), F32),
        pltpu.VMEM((GROUPS, heads, SPAN), F32),
        pltpu.VMEM((GROUPS, heads, SPAN), F32),
        pltpu.VMEM((GROUPS, SPAN, 128), F32),
        pltpu.VMEM((GROUPS, SPAN, 128), BF16),
        pltpu.VMEM((GROUPS, SPAN, 128), BF16),
        pltpu.VMEM((GROUPS, SPAN, 128), BF16),
        pltpu.VMEM((GROUPS, STATE, SPAN), BF16),
        pltpu.VMEM((GROUPS, SPAN, SPAN), F32),
        pltpu.VMEM((128, channels), BF16),
        pltpu.VMEM((STATE, width), F32),
        pltpu.VMEM((GROUPS, STATE, width), BF16),
        pltpu.VMEM((CHUNKS, STATE, width), BF16),
        pltpu.VMEM((CHUNKS, supers, slice_rows, width), BF16),
        pltpu.VMEM((CHUNKS, supers, slice_rows, width), BF16),
        pltpu.VMEM((CHUNKS, STATE, width), BF16),
        pltpu.VMEM((supers, 16, 128), BF16),
        pltpu.VMEM((max(supers, 8), channels), F32),
        pltpu.VMEM((GROUPS, SPAN, channels), F32),
        pltpu.VMEM((SPAN, width), BF16),
        pltpu.VMEM((GROUPS, SPAN, channels), F32),
        pltpu.VMEM((GROUPS, SPAN, 128), F32),
        pltpu.VMEM((GROUPS, CHUNKS, SPAN, width), BF16),
        pltpu.VMEM((GROUPS, CHUNKS, SPAN, width), BF16),
        dma((CHUNKS + 1,)), dma, dma((GROUPS,)), dma((CHUNKS + 1,)), dma((CHUNKS + 1,)),
        dma((GROUPS, CHUNKS)), dma((GROUPS, CHUNKS)),
        dma((GROUPS,)), dma((GROUPS,)),
        dma((GROUPS,)), dma((GROUPS,)),
        dma((supers,)), dma((supers,)),
        dma((CHUNKS, supers)), dma((CHUNKS, supers)),
        dma((CHUNKS, supers)), dma((CHUNKS, supers)),
        dma((GROUPS, CHUNKS)), dma((GROUPS, CHUNKS)),
        pltpu.SemaphoreType.REGULAR((supers.bit_length() - 1,)), pltpu.SemaphoreType.REGULAR, dma((6,)),
    ]
    mixed = pl.pallas_call(
        partial(body, heads=heads, supers=supers),
        out_shape=jax.ShapeDtypeStruct((rows, inner), BF16),
        in_specs=[hbm] * 9,
        out_specs=hbm,
        scratch_shapes=scratch,
        compiler_params=pltpu.CompilerParams(
            collective_id=0, has_side_effects=True, vmem_limit_bytes=61 * 2**20
        ),
        name="layer",
    )(
        values_in, gate_in, factors_in, *small
    )
    strips = 4
    return pl.pallas_call(
        partial(move, strips),
        out_shape=jax.ShapeDtypeStruct((rows, inner), BF16),
        in_specs=[hbm],
        out_specs=hbm,
        scratch_shapes=[pltpu.VMEM((rows, inner), BF16), dma((strips,)), dma((strips,))],
        name="move",
    )(mixed)


def solution(mesh):
    rows = P(("seq", "head"), None)
    placed = (rows, P(("seq", "head"), None, None, None), rows, rows, P(), P(), P(), P(), P())
    return jax.shard_map(local, mesh=mesh, in_specs=placed, out_specs=rows, check_vma=False)
```

```python
from functools import partial

import jax
import jax.numpy as jnp
from jax import lax
from jax.experimental import pallas as pl
from jax.experimental.pallas import tpu as pltpu
from jax.sharding import PartitionSpec as P

HEAD_DIM = 64
STATE = 256
GROUPS = 8
SPAN = 128
CONV = 4
CHUNKS = 4
AHEAD = 4
LANES = 256
F32 = jnp.float32
BF16 = jnp.bfloat16
MESH = pl.DeviceIdType.MESH


def silu(value):
    return value * pl.reciprocal(1.0 + jnp.exp(-value))


def silu_wide(value):
    inner = value * pl.reciprocal(1.0 + jnp.exp(jnp.minimum(-value, 87.0)))
    return jnp.where(value < -87.0, 0.0, inner)


def softplus_below_zero(value):
    e = jnp.exp(value)
    z = e / (2.0 + e)
    q = z * z
    series = 1.0 / 15.0
    for odd in (13.0, 11.0, 9.0, 7.0, 5.0, 3.0, 1.0):
        series = series * q + 1.0 / odd
    return 2.0 * z * series


def split_columns(rows):
    heads = rows.shape[0]
    high = rows.astype(BF16).astype(F32)
    middle = (rows - high).astype(BF16).astype(F32)
    low = rows - high - middle
    parts = [high, middle, low]
    if 128 > 3 * heads:
        parts.append(jnp.zeros((128 - 3 * heads, rows.shape[1]), F32))
    return jnp.transpose(jnp.concatenate(parts, axis=0)).astype(BF16)


def convolved(current, before, taps):
    padded = jnp.concatenate([before, current], axis=0)
    total = padded[5 : 5 + SPAN] * taps[0:1]
    for offset in range(1, CONV):
        total = total + padded[5 + offset : 5 + offset + SPAN] * taps[offset : offset + 1]
    return silu(total).astype(BF16)


def body(
    values_hbm, gate_hbm, fac_hbm, step_hbm, conv_v_hbm, conv_f_hbm, decay_hbm, skip_hbm, gain_hbm,
    out_hbm,
    step_in, conv_v, conv_f, decay, skip, gain, out, gate, tail_v, tail_f, raw_v, raw_f, signal, b_rows, c_rows, stp_send, stp_recv,
    head_col, skip_row, step_t, run_t, run_c, w_s, t_s, g_s, b_t, scores, expander,
    state, local_entry, s_send, st_recv, e_send, e_recv, d_recv, d_wide,
    part, weighted, gated, squares, y_send, y_recv,
    own_sem, gate_sem, out_sem, tail_ss, tail_rs,
    sig_ss, sig_rs, fac_ss, fac_rs, stp_ss, stp_rs, d_ss, d_rs,
    st_ss, st_rs, e_ss, e_rs, y_ss, y_rs, met, all_met, small_sem,
    *, heads, supers,
):
    channels = heads * HEAD_DIM
    width = channels // CHUNKS
    chunk_heads = heads // CHUNKS
    slice_rows = STATE // supers
    lanes = min(LANES, width)

    seq, col = lax.axis_index("seq"), lax.axis_index("head")
    core = lax.rem(seq, 2)
    mine = seq // 2
    me = core * 4 + col
    place = mine * GROUPS + me

    def owner(k):
        return (mine * 2 + k // 4, lax.rem(k, 4))

    def column(j):
        return (j * 2 + core, col)

    def anywhere(index):
        k = lax.rem(index, GROUPS)
        return ((index // GROUPS) * 2 + k // 4, lax.rem(k, 4))

    def other(j):
        return lax.rem(me + j, GROUPS)

    def other_super(j):
        return lax.rem(mine + j, supers)

    following = column(other_super(1))
    previous = column(other_super(supers - 1))

    def columns_of_chunk(g, c):
        return pl.ds(pl.multiple_of(g * channels + c * width, width), width)

    def own_copy(c):
        return pltpu.make_async_copy(
            values_hbm.at[:, columns_of_chunk(me, c)], raw_v.at[me, c], own_sem.at[c]
        )

    own_factors = pltpu.make_async_copy(fac_hbm.at[:, me], raw_f.at[me], own_sem.at[CHUNKS])
    gate_copy = pltpu.make_async_copy(gate_hbm, gate, gate_sem)

    def remote(src, dst, ss, rs, device):
        return pltpu.make_async_remote_copy(
            src_ref=src, dst_ref=dst, send_sem=ss, recv_sem=rs, device_id=device, device_id_type=MESH
        )

    def sig_out(g, c):
        return remote(
            values_hbm.at[:, columns_of_chunk(g, c)], raw_v.at[me, c], sig_ss.at[g, c], sig_rs.at[me, c], owner(g)
        )

    def sig_in(k, c):
        return remote(
            values_hbm.at[:, columns_of_chunk(k, c)], raw_v.at[k, c], sig_ss.at[k, c], sig_rs.at[k, c], owner(k)
        )

    def fac_out(g):
        return remote(fac_hbm.at[:, g], raw_f.at[me], fac_ss.at[g], fac_rs.at[me], owner(g))

    def fac_arrive(k):
        return remote(fac_hbm.at[:, k], raw_f.at[k], fac_ss.at[k], fac_rs.at[k], owner(k))

    last_rows = pl.ds(SPAN - 16, 16)

    def tail_v_copy(c):
        return remote(
            raw_v.at[GROUPS - 1, c, last_rows], tail_v.at[c], tail_ss.at[c], tail_rs.at[c], following
        )

    tail_f_copy = remote(
        raw_f.at[GROUPS - 1, last_rows], tail_f, tail_ss.at[CHUNKS], tail_rs.at[CHUNKS], following
    )

    def stp_out(g):
        return remote(stp_send.at[g], stp_recv.at[me], stp_ss.at[g], stp_rs.at[me], owner(g))

    def stp_arrive(k):
        return remote(stp_send.at[k], stp_recv.at[k], stp_ss.at[k], stp_rs.at[k], owner(k))

    def d_out(j):
        return remote(
            g_s.at[GROUPS - 1, pl.ds(SPAN - 16, 16)], d_recv.at[mine], d_ss.at[j], d_rs.at[mine], column(j)
        )

    def d_arrive(j):
        return remote(
            g_s.at[GROUPS - 1, pl.ds(SPAN - 16, 16)], d_recv.at[j], d_ss.at[j], d_rs.at[j], column(j)
        )

    def part_of(j):
        return pl.ds(pl.multiple_of(j * slice_rows, slice_rows), slice_rows)

    def st_out(j, c):
        return remote(
            s_send.at[c, part_of(j)], st_recv.at[c, mine], st_ss.at[c, j], st_rs.at[c, mine], column(j)
        )

    def st_arrive(j, c):
        return remote(s_send.at[c, part_of(j)], st_recv.at[c, j], st_ss.at[c, j], st_rs.at[c, j], column(j))

    def e_out(j, c):
        return remote(
            e_send.at[c, j], e_recv.at[c, part_of(mine)], e_ss.at[c, j], e_rs.at[c, mine], column(j)
        )

    def e_arrive(j, c):
        return remote(e_send.at[c, j], e_recv.at[c, part_of(j)], e_ss.at[c, j], e_rs.at[c, j], column(j))

    def y_out(k, c):
        return remote(y_send.at[k, c], y_recv.at[me, c], y_ss.at[k, c], y_rs.at[me, c], owner(k))

    def y_arrive(k, c):
        return remote(y_send.at[k, c], y_recv.at[k, c], y_ss.at[k, c], y_rs.at[k, c], owner(k))

    small = [
        pltpu.make_async_copy(source, target, small_sem.at[i])
        for i, (source, target) in enumerate(
            [
                (step_hbm, step_in), (conv_v_hbm, conv_v), (conv_f_hbm, conv_f),
                (decay_hbm, decay), (skip_hbm, skip), (gain_hbm, gain),
            ]
        )
    ]
    small[0].start()
    barrier = pltpu.get_barrier_semaphore()

    @pl.loop(1, GROUPS)
    def _(j):
        pl.semaphore_signal(barrier, inc=1, device_id=owner(other(j)), device_id_type=MESH)

    pairs = [1 << d for d in range(supers.bit_length() - 1)]

    def opposite(pair):
        return column(mine + pair - 2 * pair * lax.rem(mine // pair, 2))

    @pl.when(me == 0)
    def _():
        for pair in pairs:
            pl.semaphore_signal(barrier, inc=1, device_id=opposite(pair), device_id_type=MESH)

    small[0].wait()
    for start in range(0, GROUPS * heads, 128):
        count = min(128, GROUPS * heads - start)
        turned = jnp.transpose(step_in[:, start : start + count].astype(F32)).astype(BF16)
        stp_send[start // heads : (start + count) // heads] = turned.reshape(count // heads, heads, SPAN)

    pl.semaphore_wait(barrier, GROUPS - 1 + jnp.where(me == 0, len(pairs), 0))

    @pl.loop(1, GROUPS)
    def _(j):
        stp_out(other(j)).start()

    @pl.loop(1, GROUPS)
    def _(j):
        fac_out(other(j)).start()

    for c in range(AHEAD):

        @pl.loop(1, GROUPS)
        def _(j):
            sig_out(other(j), c).start()

    own_factors.start()
    for copy in small[1:]:
        copy.start()
    for c in range(CHUNKS):
        own_copy(c).start()
    gate_copy.start()

    stp_recv[me] = stp_send[me]

    def turn_row(row):
        for start in range(0, GROUPS * heads, 128):
            count = min(128, GROUPS * heads - start)
            head_col[start : start + count, :] = jnp.transpose(
                jnp.broadcast_to(row[:, start : start + count], (128, count))
            )
        return head_col[pl.ds(pl.multiple_of(me * heads, heads), heads), :]

    @pl.when(me == 0)
    def _():
        for d, pair in enumerate(pairs):
            pl.semaphore_signal(met.at[d], inc=1, device_id=opposite(pair), device_id_type=MESH)
            pl.semaphore_wait(met.at[d], 1)

        @pl.loop(1, GROUPS)
        def _(j):
            pl.semaphore_signal(all_met, inc=1, device_id=owner(other(j)), device_id_type=MESH)

    slot = lax.broadcasted_iota(jnp.int32, (128, channels), 0)
    channel = lax.broadcasted_iota(jnp.int32, (128, channels), 1)
    hit = jnp.zeros((128, channels), F32)
    for piece in range(3):
        hit = jnp.where(slot == channel // HEAD_DIM + piece * heads, 1.0, hit)
    expander[...] = hit.astype(BF16)

    def expand(columns, c, lb):
        return jnp.dot(
            columns, expander[:, c * width + lb : c * width + lb + lanes], preferred_element_type=F32
        )

    for copy in small[1:]:
        copy.wait()
    skip_columns = split_columns(turn_row(skip[...]))
    for lb in range(0, channels, lanes):
        skip_row[:, lb : lb + lanes] = expand(skip_columns[0:16, :], 0, lb)[0:8]
    rate = jnp.exp(turn_row(decay[...]))

    def tail_before(rows):
        return jnp.where(mine > 0, rows.astype(F32), 0.0)

    def signal_of(k, c, before):
        for lb in range(0, width, lanes):
            here = slice(lb, lb + lanes)
            taps = conv_v[:, pl.ds(pl.multiple_of(me * channels + c * width + lb, lanes), lanes)]
            signal[k, c, :, here] = convolved(
                raw_v[k, c, :, here].astype(F32), before(here), taps.astype(F32)
            )

    def factors_of(k, before):
        for part_index, target in ((0, b_rows), (1, c_rows)):
            taps = conv_f[:, me, part_index, :].astype(F32)
            target[k] = convolved(raw_f[k, :, part_index, :].astype(F32), before(part_index), taps)

    @pl.loop(1, GROUPS)
    def _(j):
        stp_arrive(other(j)).wait_recv()

    steps = softplus_below_zero(stp_recv[...].astype(F32))
    step_t[...] = steps
    falls = (steps * rate[None]).reshape(GROUPS * heads, SPAN)
    upto = (
        lax.broadcasted_iota(jnp.int32, (SPAN, SPAN), 0)
        <= lax.broadcasted_iota(jnp.int32, (SPAN, SPAN), 1)
    ).astype(F32)
    run_t[...] = -jnp.dot(
        falls, upto, preferred_element_type=F32, precision=lax.Precision.HIGHEST
    ).reshape(GROUPS, heads, SPAN)

    def columns_of(k, prior):
        running = run_t[k]
        ending = running[:, SPAN - 1 : SPAN]
        w_s[k] = split_columns(jnp.exp(ending - running) * step_t[k])
        t_s[k] = split_columns(jnp.exp(running))
        g_s[k] = split_columns(jnp.exp(running + prior))
        run_c[k] = jnp.transpose(
            jnp.concatenate([running, jnp.zeros((128 - heads, SPAN), F32)], axis=0)
        )
        return prior + ending

    lax.fori_loop(0, GROUPS, columns_of, jnp.zeros((heads, 1), F32))

    @pl.when(me != 0)
    def _():
        pl.semaphore_wait(all_met, 1)

    @pl.loop(1, supers)
    def _(j):
        d_out(other_super(j)).start()

    d_recv[mine] = g_s[GROUPS - 1, SPAN - 16 : SPAN, :]

    @pl.loop(1, GROUPS)
    def _(j):
        fac_arrive(other(j)).wait_recv()

    own_factors.wait()
    tail_f_copy.start()

    causal = lax.broadcasted_iota(jnp.int32, (SPAN, SPAN), 0) >= lax.broadcasted_iota(
        jnp.int32, (SPAN, SPAN), 1
    )

    def scores_of(k):
        turned = jnp.transpose(b_rows[k].astype(F32)).astype(BF16)
        b_t[k] = turned
        scores[k] = jnp.where(causal, jnp.dot(c_rows[k], turned, preferred_element_type=F32), 0.0)

    @pl.loop(1, GROUPS)
    def _(k):
        factors_of(k, lambda i: raw_f[k - 1, SPAN - 8 : SPAN, i, :].astype(F32))
        scores_of(k)

    tail_f_copy.wait_recv()
    factors_of(0, lambda i: tail_before(tail_f[:, i, :])[8:16])
    scores_of(0)

    def wait_chunk(c):
        @pl.loop(1, GROUPS)
        def _(j):
            sig_out(other(j), c).wait_send()
            if c + AHEAD < CHUNKS:
                sig_out(other(j), c + AHEAD).start()

        @pl.loop(1, GROUPS)
        def _(j):
            sig_in(other(j), c).wait_recv()

        own_copy(c).wait()
        tail_v_copy(c).start()

        @pl.loop(1, GROUPS)
        def _(k):
            signal_of(k, c, lambda here: raw_v[k - 1, c, SPAN - 16 : SPAN, here].astype(F32)[8:16])

        tail_v_copy(c).wait_recv()
        signal_of(0, c, lambda here: tail_before(tail_v[c, :, here])[8:16])

    def accumulate(c):
        state[...] = jnp.zeros_like(state)

        @pl.loop(0, GROUPS)
        def _(k):
            for lb in range(0, width, lanes):
                here = slice(lb, lb + lanes)
                weight = expand(w_s[k], c, lb)
                weighted[:, here] = (weight * signal[k, c, :, here].astype(F32)).astype(BF16)
                ending = expand(t_s[k, SPAN - 16 : SPAN, :], c, lb)[15:16]
                held = state[:, here]
                local_entry[k, :, here] = held.astype(BF16)
                state[:, here] = held * ending + jnp.dot(
                    b_t[k], weighted[:, here], preferred_element_type=F32
                )

        s_send[c] = state[...].astype(BF16)

        @pl.loop(1, supers)
        def _(j):
            st_out(other_super(j), c).start()

        st_recv[c, mine] = s_send[c, part_of(mine), :]

    def inside(c):
        low_half = lax.broadcasted_iota(jnp.int32, (SPAN, 128), 1) < HEAD_DIM

        @pl.loop(0, GROUPS)
        def _(k):
            for pair in range(chunk_heads // 2):
                here = slice(pair * 128, pair * 128 + 128)
                there = slice(c * width + pair * 128, c * width + pair * 128 + 128)
                mixes = []
                for h in (c * chunk_heads + 2 * pair, c * chunk_heads + 2 * pair + 1):
                    gap = run_c[k, :, h : h + 1] - run_t[k, h : h + 1, :]
                    mixes.append(
                        (jnp.exp(jnp.minimum(gap, 0.0)) * step_t[k, h : h + 1, :] * scores[k]).astype(BF16)
                    )
                values = signal[k, c, :, here].astype(F32)
                both = jnp.concatenate(
                    [
                        jnp.where(low_half, values, 0.0).astype(BF16),
                        jnp.where(low_half, 0.0, values).astype(BF16),
                    ],
                    axis=0,
                )
                part[k, :, there] = (
                    jnp.dot(jnp.concatenate(mixes, axis=1), both, preferred_element_type=F32)
                    + skip_row[0:1, there] * values
                )
            for lb in range(0, width, lanes):
                there = slice(c * width + lb, c * width + lb + lanes)
                held = jnp.dot(
                    c_rows[k], local_entry[k, :, lb : lb + lanes], preferred_element_type=F32
                )
                part[k, :, there] = part[k, :, there] + expand(t_s[k], c, lb) * held

    def exchange(c):
        if c == 0:

            @pl.loop(1, supers)
            def _(j):
                d_arrive(other_super(j)).wait_recv()

            for j in range(supers):
                d_wide[j : j + 1, :] = jnp.dot(
                    d_recv[j], expander[...], preferred_element_type=F32
                )[15:16]

        @pl.loop(1, supers)
        def _(j):
            st_arrive(other_super(j), c).wait_recv()

        entry = jnp.zeros((slice_rows, width), F32)
        for j in range(supers):
            e_send[c, j] = entry.astype(BF16)
            if j + 1 < supers:
                entry = entry * d_wide[j : j + 1, c * width : (c + 1) * width] + st_recv[c, j].astype(F32)

        @pl.loop(1, supers)
        def _(j):
            e_out(other_super(j), c).start()

        e_recv[c, part_of(mine), :] = e_send[c, mine]

    def results(c):
        @pl.loop(1, supers)
        def _(j):
            e_arrive(other_super(j), c).wait_recv()

        def result_of(k, target):
            for lb in range(0, width, lanes):
                there = slice(c * width + lb, c * width + lb + lanes)
                held = jnp.dot(
                    c_rows[k], e_recv[c, :, lb : lb + lanes], preferred_element_type=F32
                )
                target[:, lb : lb + lanes] = (
                    part[k, :, there] + expand(g_s[k], c, lb) * held
                ).astype(BF16)

        @pl.loop(1, GROUPS)
        def _(j):
            k = other(j)
            result_of(k, y_send.at[k, c])
            y_out(k, c).start()

        result_of(me, y_recv.at[me, c])

    def out_copy(k):
        columns = pl.ds(pl.multiple_of(k * channels, channels), channels)
        return pltpu.make_async_copy(out.at[:, columns], out_hbm.at[:, columns], out_sem.at[k])

    def finish(c):
        if c == 0:
            gate_copy.wait()

        @pl.loop(0, GROUPS)
        def _(j):
            k = other(GROUPS - j)

            @pl.when(j > 0)
            def _():
                y_arrive(k, c).wait_recv()

            total = jnp.zeros((SPAN, 128), F32)
            if c > 0:
                total = squares[k]
            for lb in range(0, width, lanes):
                here = pl.ds(pl.multiple_of(k * channels + c * width + lb, lanes), lanes)
                value = y_recv[k, c, :, lb : lb + lanes].astype(F32) * silu_wide(
                    gate[:, here].astype(F32)
                )
                there = slice(c * width + lb, c * width + lb + lanes)
                gated[k, :, there] = value * gain[k, :, there]
                square = value * value
                for start in range(0, lanes, 128):
                    total = total + square[:, start : start + 128]
            if c + 1 < CHUNKS:
                squares[k] = total
            else:
                mean = jnp.sum(total, axis=1, keepdims=True) * (1.0 / channels)
                inverse = lax.rsqrt(mean + 1e-05)
                for lb in range(0, channels, LANES):
                    here = pl.ds(pl.multiple_of(k * channels + lb, LANES), LANES)
                    out[:, here] = (
                        gated[k, :, lb : lb + LANES] * inverse
                    ).astype(BF16)
                out_copy(k).start()

    wait_chunk(0)
    accumulate(0)
    inside(0)
    exchange(0)
    for c in range(1, CHUNKS):
        wait_chunk(c)
        accumulate(c)
        results(c - 1)
        inside(c)
        exchange(c)
    results(CHUNKS - 1)
    for c in range(CHUNKS):
        finish(c)

    tail_f_copy.wait_send()
    for c in range(CHUNKS):
        tail_v_copy(c).wait_send()

    @pl.loop(1, GROUPS)
    def _(j):
        g = other(j)
        stp_out(g).wait_send()
        fac_out(g).wait_send()
        for c in range(CHUNKS):
            y_out(g, c).wait_send()

    @pl.loop(1, supers)
    def _(j):
        peer = other_super(j)
        d_out(peer).wait_send()
        for c in range(CHUNKS):
            st_out(peer, c).wait_send()
            e_out(peer, c).wait_send()

    @pl.loop(0, GROUPS)
    def _(j):
        out_copy(other(j)).wait()


def move(strips, source, target, held, in_sem, out_sem):
    high = held.shape[0] // strips
    reads, writes = [], []
    for i in range(strips):
        here = pl.ds(i * high, high)
        reads.append(pltpu.make_async_copy(source.at[here], held.at[here], in_sem.at[i]))
        writes.append(pltpu.make_async_copy(held.at[here], target.at[here], out_sem.at[i]))
    for read in reads:
        read.start()
    for read, write in zip(reads, writes):
        read.wait()
        write.start()
    for write in writes:
        write.wait()


def local(
    values_in, factors_in, step_raw, gate_in, conv_values, conv_factors, decay_log, skip_gain, norm_gain
):
    rows, inner = values_in.shape
    heads = step_raw.shape[1] // GROUPS
    channels = heads * HEAD_DIM
    width = channels // CHUNKS
    supers = lax.axis_size("seq") // 2
    slice_rows = STATE // supers

    gain = norm_gain.reshape(GROUPS, 1, channels)

    hbm = pl.BlockSpec(memory_space=pl.ANY)
    dma = pltpu.SemaphoreType.DMA
    small = [step_raw, conv_values, conv_factors, decay_log.reshape(1, -1), skip_gain.reshape(1, -1), gain]
    scratch = [pltpu.VMEM(array.shape, array.dtype) for array in small] + [
        pltpu.VMEM((SPAN, inner), BF16),
        pltpu.VMEM((SPAN, inner), BF16),
        pltpu.VMEM((CHUNKS, 16, width), BF16),
        pltpu.VMEM((16, 2, STATE), BF16),
        pltpu.VMEM((GROUPS, CHUNKS, SPAN, width), BF16),
        pltpu.VMEM((GROUPS, SPAN, 2, STATE), BF16),
        pltpu.VMEM((GROUPS, CHUNKS, SPAN, width), BF16),
        pltpu.VMEM((GROUPS, SPAN, STATE), BF16),
        pltpu.VMEM((GROUPS, SPAN, STATE), BF16),
        pltpu.VMEM((GROUPS, heads, SPAN), BF16),
        pltpu.VMEM((GROUPS, heads, SPAN), BF16),
        pltpu.VMEM((GROUPS * heads, 128), F32),
        pltpu.VMEM((8, channels), F32),
        pltpu.VMEM((GROUPS, heads, SPAN), F32),
        pltpu.VMEM((GROUPS, heads, SPAN), F32),
        pltpu.VMEM((GROUPS, SPAN, 128), F32),
        pltpu.VMEM((GROUPS, SPAN, 128), BF16),
        pltpu.VMEM((GROUPS, SPAN, 128), BF16),
        pltpu.VMEM((GROUPS, SPAN, 128), BF16),
        pltpu.VMEM((GROUPS, STATE, SPAN), BF16),
        pltpu.VMEM((GROUPS, SPAN, SPAN), F32),
        pltpu.VMEM((128, channels), BF16),
        pltpu.VMEM((STATE, width), F32),
        pltpu.VMEM((GROUPS, STATE, width), BF16),
        pltpu.VMEM((CHUNKS, STATE, width), BF16),
        pltpu.VMEM((CHUNKS, supers, slice_rows, width), BF16),
        pltpu.VMEM((CHUNKS, supers, slice_rows, width), BF16),
        pltpu.VMEM((CHUNKS, STATE, width), BF16),
        pltpu.VMEM((supers, 16, 128), BF16),
        pltpu.VMEM((max(supers, 8), channels), F32),
        pltpu.VMEM((GROUPS, SPAN, channels), F32),
        pltpu.VMEM((SPAN, width), BF16),
        pltpu.VMEM((GROUPS, SPAN, channels), F32),
        pltpu.VMEM((GROUPS, SPAN, 128), F32),
        pltpu.VMEM((GROUPS, CHUNKS, SPAN, width), BF16),
        pltpu.VMEM((GROUPS, CHUNKS, SPAN, width), BF16),
        dma((CHUNKS + 1,)), dma, dma((GROUPS,)), dma((CHUNKS + 1,)), dma((CHUNKS + 1,)),
        dma((GROUPS, CHUNKS)), dma((GROUPS, CHUNKS)),
        dma((GROUPS,)), dma((GROUPS,)),
        dma((GROUPS,)), dma((GROUPS,)),
        dma((supers,)), dma((supers,)),
        dma((CHUNKS, supers)), dma((CHUNKS, supers)),
        dma((CHUNKS, supers)), dma((CHUNKS, supers)),
        dma((GROUPS, CHUNKS)), dma((GROUPS, CHUNKS)),
        pltpu.SemaphoreType.REGULAR((supers.bit_length() - 1,)), pltpu.SemaphoreType.REGULAR, dma((6,)),
    ]
    mixed = pl.pallas_call(
        partial(body, heads=heads, supers=supers),
        out_shape=jax.ShapeDtypeStruct((rows, inner), BF16),
        in_specs=[hbm] * 9,
        out_specs=hbm,
        scratch_shapes=scratch,
        compiler_params=pltpu.CompilerParams(
            collective_id=0, has_side_effects=True, vmem_limit_bytes=61 * 2**20
        ),
        name="layer",
    )(
        values_in, gate_in, factors_in, *small
    )
    strips = 4
    return pl.pallas_call(
        partial(move, strips),
        out_shape=jax.ShapeDtypeStruct((rows, inner), BF16),
        in_specs=[hbm],
        out_specs=hbm,
        scratch_shapes=[pltpu.VMEM((rows, inner), BF16), dma((strips,)), dma((strips,))],
        name="move",
    )(mixed)


def solution(mesh):
    rows = P(("seq", "head"), None)
    placed = (rows, P(("seq", "head"), None, None, None), rows, rows, P(), P(), P(), P(), P())
    return jax.shard_map(local, mesh=mesh, in_specs=placed, out_specs=rows, check_vma=False)
```
